256 devices in a mesh: tm: 8 (over y, x_hi), dp: 32 (over z, x_lo, core).
Axes of the slice: x: 4 (x_hi: 2, x_lo: 2; x = x_hi * 2 + x_lo), y: 4, z: 8, core: 2. Of those that a mesh axis runs over, the one named last changes fastest.
Arguments:
- features: bfloat16 [32, 32, 2, 8, 256], P('dp', 'tm'), may hold values from -6 to 6
- upstream: bfloat16 [32, 32, 4, 16, 128], P('dp', 'tm'), may hold values from -6 to 6
- weight_one: bfloat16 [3, 3, 3, 256, 128], replicated, may hold values from -0.078125 to 0.078125
- weight_two: bfloat16 [3, 3, 3, 128, 128], replicated, may hold values from -0.109375 to 0.109375
Outputs:
- feature_grad: bfloat16 [32, 32, 2, 8, 256], P('dp', 'tm')
- grad_one: float32 [3, 3, 3, 256, 128], P(None, None, None, 'dp')
- grad_two: float32 [3, 3, 3, 128, 128], P(None, None, None, 'dp')
The draws below stay inside these ranges and needn't reach their ends.
All inputs are finite; a program needn't handle non-finite values.
Results may differ from the reference program's by a relative error of at most 0.0049.
Values may be sent and summed in bfloat16 or wider, within the bound.
A program may use at most 64 MiB of HBM per device.

```python
import jax
import jax.numpy as jnp
from jax import lax

CIN = 256
COUT = 128
HI = 2
WI = 8
HO = 4
WO = 16
CLIPS = 32
FRAMES = 32


def level_of(key, shape, split, least, largest):
    level, own = 1.0, jax.random.fold_in(key, 6)
    for dim, parts in split:
        heights = jnp.exp(jax.random.uniform(jax.random.fold_in(own, dim), (parts,), jnp.float32, least / len(split), largest / len(split)))
        level = level * jnp.repeat(heights, shape[dim] // parts).reshape([-1 if axis == dim else 1 for axis in range(len(shape))])
    return level


def bell_draw(own_key, shape, deviation, limit, shards=(), kind=jnp.bfloat16):
    array = deviation * jax.random.normal(own_key, shape, jnp.float32)
    if shards:
        array = array * level_of(own_key, shape, shards, -0.22, 0.18)
    return jnp.clip(array, -limit, limit).astype(kind)


def setup_inputs(seed: int = 0) -> dict:
    arg_keys = jax.random.split(jax.random.key(seed), 5)
    return {
        "features": bell_draw(arg_keys[0], (CLIPS, FRAMES, HI, WI, CIN), 1.0, 6.0, ((0, 32), (1, 8))),
        "upstream": bell_draw(arg_keys[1], (CLIPS, FRAMES, HO, WO, COUT), 1.0, 6.0, ((0, 32), (1, 8))),
        "weight_one": bell_draw(arg_keys[2], (3, 3, 3, CIN, COUT), (27 * CIN) ** -0.5, 0.078125),
        "weight_two": bell_draw(arg_keys[3], (3, 3, 3, COUT, COUT), (27 * COUT) ** -0.5, 0.109375),
    }


def upsample(values):
    return jnp.repeat(jnp.repeat(values, 2, axis=2), 2, axis=3)

def forward_conv(padded, kernel):
    return lax.conv_general_dilated(padded, kernel, (1, 1, 1), 'VALID', dimension_numbers=('NDHWC', 'DHWIO', 'NDHWC'), preferred_element_type=jnp.float32)

def kernel_grad(padded, cotangent):
    return lax.conv_general_dilated(padded, cotangent, (1, 1, 1), 'VALID', dimension_numbers=('CDHWN', 'IDHWO', 'DHWNC'), preferred_element_type=jnp.float32)

def data_grad(cotangent, kernel):
    return lax.conv_general_dilated(cotangent, kernel[::-1, ::-1, ::-1], (1, 1, 1), [(2, 2), (2, 2), (2, 2)], dimension_numbers=('NDHWC', 'DHWOI', 'NDHWC'), preferred_element_type=jnp.float32)

def pad_causal(values):
    return jnp.pad(values, ((0, 0), (2, 0), (1, 1), (1, 1), (0, 0)))

def silu_slope(pre):
    sigma = jax.nn.sigmoid(pre)
    return sigma * (1.0 + pre * (1.0 - sigma))

def pool_pairs(values):
    shape = values.shape
    return values.reshape(shape[0], shape[1], shape[2] // 2, 2, shape[3] // 2, 2, shape[4]).sum(axis=(3, 5))

def reference(features, upstream, weight_one, weight_two):
    count = upstream.shape[0] * upstream.shape[1] * upstream.shape[2] * upstream.shape[3]
    factor = 1.0 / count ** 0.5

    def one_clip(pair):
        feats, cotangent = pair
        cotangent = cotangent[None]
        padded = pad_causal(upsample(feats[None]))
        pre = forward_conv(padded, weight_one)
        hidden = jax.nn.silu(pre).astype(jnp.bfloat16)
        grad_second = kernel_grad(pad_causal(hidden), cotangent)
        back = data_grad(cotangent, weight_two)[:, 2:, 1:-1, 1:-1]
        dpre = (back * silu_slope(pre)).astype(jnp.bfloat16)
        grad_first = kernel_grad(padded, dpre)
        up_grad = data_grad(dpre, weight_one)[:, 2:, 1:-1, 1:-1]
        return (pool_pairs(up_grad).astype(jnp.bfloat16)[0], grad_first, grad_second)
    results = lax.map(one_clip, (features, upstream))
    return (results[0], lax.optimization_barrier(jnp.sum(results[1], axis=0)) * factor, lax.optimization_barrier(jnp.sum(results[2], axis=0)) * factor)
```

```python
import jax
import jax.numpy as jnp
import numpy as np
from jax import lax
from jax.experimental import pallas as pl
from jax.experimental.pallas import tpu as pltpu
from jax.sharding import PartitionSpec as P

MESH = pl.DeviceIdType.MESH
F32, BF16 = jnp.float32, jnp.bfloat16

NZ, NX, NY, NTM = 8, 4, 4, 8
TILES = 24
HALF = 12


def tables():
    select = np.zeros((256, 576), np.float32)
    for f in range(4):
        for r in range(4):
            for s in range(16):
                for b in range(3):
                    for e in range(3):
                        rr, ss = r + b - 1, s + e - 1
                        if 0 <= rr < 4 and 0 <= ss < 16:
                            select[f * 64 + r * 16 + s, (b * 3 + e) * 64 + f * 16 + rr // 2 * 8 + ss // 2] = 1
    order_one = np.zeros((256, 256), np.float32)
    order_two = np.zeros((512, 384), np.float32)
    for core in range(2):
        for x_lo in range(2):
            for z in range(8):
                d = (core * 2 + x_lo) * 8 + z
                dp = z * 4 + x_lo * 2 + core
                for k in range(8):
                    order_one[d * 8 + k, dp * 8 + k] = 1
                for a in range(3):
                    for k in range(4):
                        order_two[d * 16 + a * 4 + k, a * 128 + dp * 4 + k] = 1
    return [jnp.asarray(m, BF16) for m in (select, select.T, order_one, order_two)]


def dot(a, b):
    return jnp.dot(a, b, preferred_element_type=F32)


def dot_nt(a, b):
    return lax.dot_general(a, b, (((1,), (1,)), ((), ())), preferred_element_type=F32)


def slots(z, t):
    if z < 4:
        return (0, 2 * z + t) if t < 2 else (1, z)
    return (0, 4 + z) if t == 0 else (1, 4 + 2 * (z - 4) + t - 1)


def kernel(
    f_ref, u_ref, w1_ref, w2_ref, up_ref, pool_ref, ord1_ref, ord2_ref,
    fg_ref, g1_ref, g2_ref,
    fh, uh, ystk, u9, hid, slope, dpre, p9,
    ra, rb, ra0, rb0, ra1, rb1, sa, sb, ra2, rb2, zb, rz, share, gath,
    s_halo, r_halo, s_a0, r_a0, s_b0, r_b0, s_a1, r_a1, s_b1, r_b1, s_a2, r_a2, s_b2, r_b2, s_z, r_z, s_g, r_g,
):
    tm, dp = lax.axis_index("tm"), lax.axis_index("dp")
    y, x_hi = tm // 2, tm % 2
    z, x_lo, core = dp // 4, (dp // 2) % 2, dp % 2
    x = x_lo * 2 + x_hi

    def at(xx=x, yy=y, zz=z, cc=core):
        return {"tm": yy * 2 + xx % 2, "dp": zz * 4 + (xx // 2) * 2 + cc}

    def at_tm(t):
        return {"tm": t, "dp": dp}

    barrier = pltpu.get_barrier_semaphore()
    peers = [at_tm((tm + k) % NTM) for k in range(1, NTM)]
    peers += [at(zz=(z + k) % NZ) for k in range(1, NZ)]
    peers += [at(cc=1 - core)]
    other = (1 - x_lo) * 2
    peers += [at(xx=other), at(xx=other + 1)]
    for peer in peers:
        pl.semaphore_signal(barrier, inc=1, device_id=peer, device_id_type=MESH)
    pl.semaphore_wait(barrier, len(peers))

    def send(src, dst, ssem, rsem, to):
        copy = pltpu.make_async_remote_copy(
            src_ref=src, dst_ref=dst, send_sem=ssem, recv_sem=rsem, device_id=to, device_id_type=MESH
        )
        copy.start()
        return copy

    nxt, prv = at_tm((tm + 1) % NTM), at_tm((tm + NTM - 1) % NTM)
    halo = [
        send(f_ref, fh.at[pl.ds(0, 64)], s_halo.at[0], r_halo.at[0], nxt),
        send(f_ref.at[pl.ds(0, 32)], fh.at[pl.ds(128, 32)], s_halo.at[1], r_halo.at[1], prv),
        send(u_ref, uh.at[pl.ds(0, 256)], s_halo.at[2], r_halo.at[2], prv),
    ]
    fh[64:128, :] = f_ref[...]
    column = lax.broadcasted_iota(jnp.int32, (256, 128), 0) % 16

    def shifted(block, first):
        wide = block.astype(F32)
        back_one = jnp.where(column == 15, 0.0, pltpu.roll(wide, 255, 0)).astype(BF16)
        on_one = jnp.where(column == 0, 0.0, pltpu.roll(wide, 1, 0)).astype(BF16)
        zero = jnp.zeros((4, 16, 128), BF16)
        for e, v in enumerate((back_one, block, on_one)):
            v = v.reshape(4, 64, 128)
            for b in range(3):
                tap = slice((b * 3 + e) * 128, (b * 3 + e + 1) * 128)
                if b == 0:
                    rows = jnp.concatenate([v[:, 16:], zero], axis=1)
                elif b == 1:
                    rows = v
                else:
                    rows = jnp.concatenate([zero, v[:, :48]], axis=1)
                u9[first : first + 256, tap] = rows.reshape(256, 128)

    shifted(u_ref[...], 0)

    halo[0].wait()
    halo[1].wait()

    @pl.when(tm == 0)
    def _():
        fh[0:64, :] = jnp.zeros((64, 256), BF16)

    @pl.when(tm == NTM - 1)
    def _():
        fh[128:160, :] = jnp.zeros((32, 256), BF16)

    cat = jnp.concatenate([fh[0:128, :], fh[16:144, :], fh[32:160, :]], axis=1)
    for be in range(9):
        prod = dot(cat, w1_ref[:, be].reshape(768, 128))
        high = prod.astype(BF16)
        low = (prod - high.astype(F32)).astype(BF16)
        for blk in range(2):
            ystk[blk, 0, be * 64 : be * 64 + 64, :] = high[blk * 64 : blk * 64 + 64]
            ystk[blk, 1, be * 64 : be * 64 + 64, :] = low[blk * 64 : blk * 64 + 64]
    for blk in range(2):
        pre = dot(up_ref[...], ystk[blk, 0]) + dot(up_ref[...], ystk[blk, 1])
        sigma = 1.0 / (1.0 + jnp.exp(-pre))
        hid[blk * 256 : blk * 256 + 256, :] = (pre * sigma).astype(BF16)
        slope[blk * 256 : blk * 256 + 256, :] = sigma * (1.0 + pre * (1.0 - sigma))

    halo[2].wait()

    @pl.when(tm == NTM - 1)
    def _():
        uh[...] = jnp.zeros((256, 128), BF16)

    shifted(uh[...], 256)
    back = jnp.zeros((384, 128), F32)
    for a in range(3):
        kern = jnp.concatenate([w2_ref[a, be] for be in range(9)], axis=1)
        back += dot_nt(u9[(2 - a) * 64 : (2 - a) * 64 + 384, :], kern)
    dpre[0:384, :] = (back * slope[128:512, :]).astype(BF16)
    dpre[384:512, :] = jnp.zeros((128, 128), BF16)
    for blk in range(2):
        pooled = dot(pool_ref[...], dpre[blk * 256 : blk * 256 + 256, :]).astype(BF16)
        for be in range(9):
            p9[blk * 64 : blk * 64 + 64, be * 128 : be * 128 + 128] = pooled[be * 64 : be * 64 + 64]

    def put(tile, value):
        j, t = tile // 3, tile % 3
        yy, hh = j // 2, j % 2
        for c in range(2):
            for lo in range(2):
                for zz in range(8):
                    route, slot = slots(zz, t)
                    v = value[(c * 2 + lo) * 8 + zz]
                    if route == 0:
                        ra[c, lo * 2 + hh, yy, slot] = v
                    else:
                        rb[c, yy, lo * 2 + hh, slot] = v

    turned = dot_nt(ord2_ref[...], jnp.concatenate([hid[a * 64 : a * 64 + 256, :] for a in range(3)], axis=1)).astype(BF16)
    for be in range(9):
        two = dot(turned, u9[0:256, be * 128 : be * 128 + 128])
        put(14 + be, two.astype(BF16).reshape(32, 16, 128))
    units = []
    for a in range(3):
        feats = dot_nt(ord1_ref[...], fh[(2 + a) * 16 : (2 + a) * 16 + 64, :]).astype(BF16)
        for be in range(9):
            units.append(dot(feats, p9[0:64, be * 128 : be * 128 + 128]).reshape(32, 8, 128))
            if len(units) == 2:
                put((a * 9 + be) // 2, jnp.concatenate(units, axis=1).astype(BF16))
                units = []
    units.append(jnp.zeros((32, 8, 128), F32))
    put(13, jnp.concatenate(units, axis=1).astype(BF16))
    put(23, jnp.zeros((32, 16, 128), BF16))

    mate = at(cc=1 - core)
    first = []
    for k in (1, 2, 3, 0):
        xd, yd = (x + k) % NX, (y + k) % NY
        first.append((
            k,
            send(ra.at[1 - core, xd], ra0.at[xd], s_a0.at[k], r_a0.at[k], mate),
            send(rb.at[1 - core, yd], rb0.at[yd], s_b0.at[k], r_b0.at[k], mate),
        ))

    result = jnp.zeros((64, 256), F32)
    for a in range(3):
        kern = jnp.concatenate([w1_ref[a, be] for be in range(9)], axis=1)
        result += dot_nt(p9[(2 - a) * 16 : (2 - a) * 16 + 64, :], kern)
    fg_ref[...] = result.astype(BF16)

    second_a, second_b = [], []
    for k, copy_a, copy_b in first:
        xd, yd = (x + k) % NX, (y + k) % NY
        copy_a.wait_recv()
        ra[core, xd] = (ra[core, xd].astype(F32) + ra0[xd].astype(F32)).astype(BF16)
        if k:
            second_a.append(send(ra.at[core, xd], ra1.at[k - 1], s_a1.at[k - 1], r_a1.at[k - 1], at(xx=xd)))
        copy_b.wait_recv()
        rb[core, yd] = (rb[core, yd].astype(F32) + rb0[yd].astype(F32)).astype(BF16)
        if k:
            second_b.append(send(rb.at[core, yd], rb1.at[k - 1], s_b1.at[k - 1], r_b1.at[k - 1], at(yy=yd)))

    for copy in second_a + second_b:
        copy.wait_recv()
    sums_a = ra[core, x].astype(F32)
    sums_b = rb[core, y].astype(F32)
    for k in range(3):
        sums_a += ra1[k].astype(F32)
        sums_b += rb1[k].astype(F32)
    sa[...] = sums_a.astype(BF16)
    sb[...] = sums_b.astype(BF16)
    third = []
    for k in range(1, 4):
        xd, yd = (x + k) % NX, (y + k) % NY
        third.append(send(sa.at[yd], ra2.at[k - 1], s_a2.at[k - 1], r_a2.at[k - 1], at(yy=yd)))
        third.append(send(sb.at[xd], rb2.at[k - 1], s_b2.at[k - 1], r_b2.at[k - 1], at(xx=xd)))
    for copy in third:
        copy.wait_recv()
    ends = [sa[y].astype(F32), sb[x].astype(F32)]
    for k in range(3):
        ends[0] += ra2[k].astype(F32)
        ends[1] += rb2[k].astype(F32)
    ends = [v.astype(BF16) for v in ends]
    for zz in range(8):
        for t in range(3):
            route, slot = slots(zz, t)
            zb[zz, t * 16 : t * 16 + 16, :] = ends[route][slot]
    fourth = []
    for k in range(1, 8):
        zd = (z + k) % NZ
        fourth.append(send(zb.at[zd], rz.at[k - 1], s_z.at[k - 1], r_z.at[k - 1], at(zz=zd)))
    for copy in fourth:
        copy.wait_recv()
    total = zb[z].astype(F32)
    for k in range(7):
        total += rz[k].astype(F32)
    total *= 1.0 / 256.0
    share[...] = total
    gath[tm] = total
    fifth = []
    for k in range(1, 8):
        fifth.append(send(share, gath.at[tm], s_g.at[k - 1], r_g.at[k - 1], at_tm((tm + k) % NTM)))
    for copy in fifth:
        copy.wait_recv()
    for tile in range(23):
        rows = gath[tile // 3, tile % 3 * 16 : tile % 3 * 16 + 16, :]
        if tile < 14:
            g1_ref[2 * tile] = rows[0:8]
            if tile < 13:
                g1_ref[2 * tile + 1] = rows[8:16]
        else:
            for a in range(3):
                g2_ref[a * 9 + tile - 14] = rows[a * 4 : a * 4 + 4]

    for k, copy_a, copy_b in first:
        copy_a.wait_send()
        copy_b.wait_send()
    for copy in second_a + second_b + third + fourth + fifth:
        copy.wait_send()


def on_device(features, upstream, weight_one, weight_two):
    dma = pltpu.SemaphoreType.DMA
    vmem = pltpu.VMEM
    pairs = lambda n: [dma((n,)), dma((n,))]
    scratch = [
        vmem((160, 256), BF16), vmem((256, 128), BF16), vmem((2, 2, 576, 128), BF16), vmem((512, 1152), BF16),
        vmem((512, 128), BF16), vmem((512, 128), F32), vmem((512, 128), BF16), vmem((128, 1152), BF16),
        vmem((2, NX, NY, HALF, 16, 128), BF16), vmem((2, NY, NX, HALF, 16, 128), BF16),
        vmem((NX, NY, HALF, 16, 128), BF16), vmem((NY, NX, HALF, 16, 128), BF16),
        vmem((3, NY, HALF, 16, 128), BF16), vmem((3, NX, HALF, 16, 128), BF16),
        vmem((NY, HALF, 16, 128), BF16), vmem((NX, HALF, 16, 128), BF16),
        vmem((3, HALF, 16, 128), BF16), vmem((3, HALF, 16, 128), BF16),
        vmem((NZ, 48, 128), BF16), vmem((NZ - 1, 48, 128), BF16),
        vmem((48, 128), F32), vmem((NTM, 48, 128), F32),
    ]
    scratch += pairs(3) + pairs(4) * 2 + pairs(3) * 4 + pairs(7) * 2
    spec = pl.BlockSpec(memory_space=pltpu.VMEM)
    fg, one, two = pl.pallas_call(
        kernel,
        out_shape=(
            jax.ShapeDtypeStruct((64, 256), BF16),
            jax.ShapeDtypeStruct((27, 8, 128), F32),
            jax.ShapeDtypeStruct((27, 4, 128), F32),
        ),
        in_specs=[spec] * 8,
        out_specs=(spec,) * 3,
        scratch_shapes=scratch,
        compiler_params=pltpu.CompilerParams(
            collective_id=0, has_side_effects=True, vmem_limit_bytes=48 * 1024 * 1024
        ),
    )(
        features.reshape(64, 256),
        upstream.reshape(256, 128),
        weight_one.reshape(3, 9, 256, 128),
        weight_two.reshape(3, 9, 128, 128),
        *tables(),
    )
    return (
        fg.reshape(features.shape),
        one.reshape(3, 3, 3, 8, 128),
        two.reshape(3, 3, 3, 4, 128),
    )


def solution(mesh):
    wide = P("dp", "tm", None, None, None)
    cut = P(None, None, None, "dp", None)
    return jax.shard_map(
        on_device, mesh=mesh, in_specs=(wide, wide, P(), P()), out_specs=(wide, cut, cut), check_vma=False
    )
```

```python
import jax
import jax.numpy as jnp
import numpy as np
from jax import lax
from jax.experimental import pallas as pl
from jax.experimental.pallas import tpu as pltpu
from jax.sharding import PartitionSpec as P

MESH = pl.DeviceIdType.MESH
F32, BF16 = jnp.float32, jnp.bfloat16

NZ, NX, NY, NTM = 8, 4, 4, 8


def tables():
    select = np.zeros((256, 576), np.float32)
    for f in range(4):
        for r in range(4):
            for s in range(16):
                for b in range(3):
                    for e in range(3):
                        rr, ss = r + b - 1, s + e - 1
                        if 0 <= rr < 4 and 0 <= ss < 16:
                            select[f * 64 + r * 16 + s, (b * 3 + e) * 64 + f * 16 + rr // 2 * 8 + ss // 2] = 1
    order_one = np.zeros((256, 256), np.float32)
    order_two = np.zeros((512, 384), np.float32)
    for core in range(2):
        for x_lo in range(2):
            for z in range(8):
                d = (core * 2 + x_lo) * 8 + z
                dp = z * 4 + x_lo * 2 + core
                for k in range(8):
                    order_one[d * 8 + k, dp * 8 + k] = 1
                for a in range(3):
                    for k in range(4):
                        order_two[d * 16 + a * 4 + k, a * 128 + dp * 4 + k] = 1
    return [jnp.asarray(m, BF16) for m in (select, select.T, order_one, order_two)]


def dot(a, b):
    return jnp.dot(a, b, preferred_element_type=F32)


def dot_nt(a, b):
    return lax.dot_general(a, b, (((1,), (1,)), ((), ())), preferred_element_type=F32)


def kernel(
    f_hbm, u_hbm, w1_hbm, w2_hbm, up_hbm, pool_hbm, ord1_hbm, ord2_hbm,
    fg_ref, g1_ref, g2_ref,
    u_ref, w1_ref, w2_ref, up_ref, pool_ref, ord1_ref, ord2_ref, s_in,
    fh, uh, um, fm, ystk, u9, u9m, hid, slope, p9, p9m, turned, away, away_in, part, part_in,
    ea, eb, la, lb, ea1, eb1, la1, lb1, sea, seb, sla, slb, ea2, eb2, la2, lb2,
    ze, zl, ze1, zl1, ge, gl, ge_in, gl_in,
    s_near, r_near, s_mate, r_mate,
    s_e1, r_e1, s_l1, r_l1, s_e2, r_e2, s_l2, r_l2, s_e3, r_e3, s_l3, r_l3, s_e4, r_e4, s_l4, r_l4,
):
    tm, dp = lax.axis_index("tm"), lax.axis_index("dp")
    y, x_hi = tm // 2, tm % 2
    z, x_lo, core = dp // 4, (dp // 2) % 2, dp % 2
    x = x_lo * 2 + x_hi

    def at(xx=x, yy=y, zz=z, cc=core):
        return {"tm": yy * 2 + xx % 2, "dp": zz * 4 + (xx // 2) * 2 + cc}

    def at_tm(t):
        return {"tm": t, "dp": dp}

    barrier = pltpu.get_barrier_semaphore()
    peers = [at_tm((tm + k) % NTM) for k in range(1, NTM)]
    peers += [at(zz=(z + k) % NZ) for k in range(1, NZ)]
    peers += [at(cc=1 - core)]
    other = (1 - x_lo) * 2
    peers += [at(xx=other), at(xx=other + 1)]
    for peer in peers:
        pl.semaphore_signal(barrier, inc=1, device_id=peer, device_id_type=MESH)

    loads = []
    order = (
        (u_hbm, u_ref), (f_hbm, fh.at[pl.ds(64, 64)]), (w1_hbm, w1_ref), (up_hbm, up_ref),
        (ord2_hbm, ord2_ref), (w2_hbm, w2_ref), (pool_hbm, pool_ref), (ord1_hbm, ord1_ref),
    )
    for i, (src, dst) in enumerate(order):
        loads.append(pltpu.make_async_copy(src, dst, s_in.at[i]))
        loads[i].start()

    sent = []

    def send(src, dst, ssem, rsem, to):
        copy = pltpu.make_async_remote_copy(
            src_ref=src, dst_ref=dst, send_sem=ssem, recv_sem=rsem, device_id=to, device_id_type=MESH
        )
        copy.start()
        sent.append(copy)
        return copy

    def shifted(block, frames, ref, first):
        n = frames * 64
        column = lax.broadcasted_iota(jnp.int32, (n, 128), 0) % 16
        wide = block.astype(F32)
        back_one = jnp.where(column == 15, 0.0, pltpu.roll(wide, n - 1, 0)).astype(BF16)
        on_one = jnp.where(column == 0, 0.0, pltpu.roll(wide, 1, 0)).astype(BF16)
        zero = jnp.zeros((frames, 16, 128), BF16)
        for e, v in enumerate((back_one, block, on_one)):
            v = v.reshape(frames, 64, 128)
            for b in range(3):
                tap = slice((b * 3 + e) * 128, (b * 3 + e + 1) * 128)
                if b == 0:
                    rows = jnp.concatenate([v[:, 16:], zero], axis=1)
                elif b == 1:
                    rows = v
                else:
                    rows = jnp.concatenate([zero, v[:, :48]], axis=1)
                ref[first : first + n, tap] = rows.reshape(n, 128)

    ystk[...] = jnp.zeros(ystk.shape, BF16)
    p9[0:32, :] = jnp.zeros((32, 1152), BF16)
    p9[96:128, :] = jnp.zeros((32, 1152), BF16)
    loads[0].wait()
    shifted(u_ref[...], 4, u9, 0)

    pl.semaphore_wait(barrier, len(peers))
    nxt, prv, mate = at_tm((tm + 1) % NTM), at_tm((tm + NTM - 1) % NTM), at(cc=1 - core)
    near = [
        send(f_hbm, fh.at[pl.ds(0, 64)], s_near.at[0], r_near.at[0], nxt),
        send(u_hbm.at[pl.ds(0, 128)], uh, s_near.at[1], r_near.at[1], prv),
    ]
    from_mate = [send(u_ref, um, s_mate.at[0], r_mate.at[0], mate)]
    from_mate[0].wait_recv()
    shifted(um[...], 4, u9m, 0)
    for i in range(1, 5):
        loads[i].wait()

    near[0].wait_recv()

    @pl.when(tm == 0)
    def _():
        fh[0:64, :] = jnp.zeros((64, 256), BF16)

    from_mate.append(send(fh.at[pl.ds(32, 96)], fm, s_mate.at[1], r_mate.at[1], mate))
    cat = jnp.concatenate([fh[0:96, :], fh[16:112, :], fh[32:128, :]], axis=1)
    for be in range(9):
        prod = dot(cat, w1_ref[:, be].reshape(768, 128))
        high = prod.astype(BF16)
        low = (prod - high.astype(F32)).astype(BF16)
        ystk[0, 0, be * 64 : be * 64 + 64, :] = high[0:64]
        ystk[0, 1, be * 64 : be * 64 + 64, :] = low[0:64]
        ystk[1, 0, be * 64 : be * 64 + 32, :] = high[64:96]
        ystk[1, 1, be * 64 : be * 64 + 32, :] = low[64:96]
    for blk, n in ((0, 256), (1, 128)):
        pre = dot(up_ref[0:n, :], ystk[blk, 0]) + dot(up_ref[0:n, :], ystk[blk, 1])
        sigma = 1.0 / (1.0 + jnp.exp(-pre))
        hid[blk * 256 : blk * 256 + n, :] = (pre * sigma).astype(BF16)
        slope[blk * 256 : blk * 256 + n, :] = sigma * (1.0 + pre * (1.0 - sigma))

    taps = jnp.concatenate([hid[a * 64 : a * 64 + 256, :] for a in range(3)], axis=1)
    away[...] = dot_nt(ord2_ref[pl.ds(pl.multiple_of((1 - core) * 256, 256), 256), :], taps).astype(BF16)
    from_mate.append(send(away, away_in, s_mate.at[2], r_mate.at[2], mate))
    turned[...] = dot_nt(ord2_ref[pl.ds(pl.multiple_of(core * 256, 256), 256), :], taps).astype(BF16)

    near[1].wait_recv()

    @pl.when(tm == NTM - 1)
    def _():
        uh[...] = jnp.zeros((128, 128), BF16)

    shifted(uh[...], 2, u9, 256)
    for i in range(5, 8):
        loads[i].wait()
    back = jnp.zeros((256, 128), F32)
    for a in range(3):
        kern = jnp.concatenate([w2_ref[a, be] for be in range(9)], axis=1)
        back += dot_nt(u9[(2 - a) * 64 : (2 - a) * 64 + 256, :], kern)
    dpre = (back * slope[128:384, :]).astype(BF16)
    pooled = dot(pool_ref[...], dpre).astype(BF16)
    for be in range(9):
        p9[32:96, be * 128 : be * 128 + 128] = pooled[be * 64 : be * 64 + 64]
    from_mate.append(send(p9.at[pl.ds(32, 64)], p9m, s_mate.at[3], r_mate.at[3], mate))

    def put_late(tile, value):
        value = value.reshape(2, 8, 16, 128)
        for lo in range(2):
            xx, yy = lo * 2 + tile // 2 % 2, tile // 4
            if tile % 2 == 0:
                la[xx, yy] = value[lo]
            else:
                lb[yy, xx] = value[lo]

    from_mate[2].wait_recv()
    for be in range(9):
        tap = slice(be * 128, be * 128 + 128)
        two = dot(turned[...], u9[0:256, tap]) + dot(away_in[...], u9m[:, tap])
        two = two.astype(BF16)
        if be == 8:
            put_late(14, two)
        else:
            two = two.reshape(2, 8, 16, 128)
            for lo in range(2):
                xx, yy = lo * 2 + be % 2, be // 2
                ea[xx, yy] = two[lo, :4]
                eb[yy, xx] = two[lo, 4:]

    def around(src_a, src_b, dst_a, dst_b, ssem, rsem, swap):
        copies = []
        for k in range(1, 4):
            xd, yd = (x + k) % NX, (y + k) % NY
            ia, ib = (yd, xd) if swap else (xd, yd)
            to_a, to_b = (at(yy=yd), at(xx=xd)) if swap else (at(xx=xd), at(yy=yd))
            copies.append(send(src_a.at[ia], dst_a.at[k - 1], ssem.at[2 * k - 2], rsem.at[2 * k - 2], to_a))
            copies.append(send(src_b.at[ib], dst_b.at[k - 1], ssem.at[2 * k - 1], rsem.at[2 * k - 1], to_b))
        return copies

    def added(own, parts, count):
        total = own.astype(F32)
        for k in range(count):
            total += parts[k].astype(F32)
        return total

    e1 = around(ea, eb, ea1, eb1, s_e1, r_e1, False)

    result = jnp.zeros((96, 256), F32)
    for a in range(3):
        kern = jnp.concatenate([w1_ref[a, be] for be in range(9)], axis=1)
        result += dot_nt(p9[(2 - a) * 16 : (2 - a) * 16 + 96, :], kern)
    part[...] = result

    from_mate[1].wait_recv()
    from_mate[3].wait_recv()
    units = []
    pools = jnp.concatenate([p9[32:96, :], p9m[...]], axis=0)
    mine = pl.ds(pl.multiple_of(core * 128, 128), 128)
    for a in range(3):
        rows = jnp.concatenate([fh[32 + a * 16 : 96 + a * 16, :], fm[a * 16 : a * 16 + 64, :]], axis=0)
        feats = dot_nt(ord1_ref[mine, :], rows).astype(BF16)
        for be in range(9):
            units.append(dot(feats, pools[:, be * 128 : be * 128 + 128]).reshape(16, 8, 128))
            if len(units) == 2:
                put_late((a * 9 + be) // 2, jnp.concatenate(units, axis=1).astype(BF16))
                units = []
    units.append(jnp.zeros((16, 8, 128), F32))
    put_late(13, jnp.concatenate(units, axis=1).astype(BF16))
    put_late(15, jnp.zeros((16, 16, 128), BF16))
    l1 = around(la, lb, la1, lb1, s_l1, r_l1, False)
    near.append(send(part.at[pl.ds(0, 32)], part_in, s_near.at[2], r_near.at[2], prv))

    for copy in e1:
        copy.wait_recv()
    sea[...] = added(ea[x], ea1, 3).astype(BF16)
    seb[...] = added(eb[y], eb1, 3).astype(BF16)
    e2 = around(sea, seb, ea2, eb2, s_e2, r_e2, True)
    for copy in l1:
        copy.wait_recv()
    sla[...] = added(la[x], la1, 3).astype(BF16)
    slb[...] = added(lb[y], lb1, 3).astype(BF16)
    l2 = around(sla, slb, la2, lb2, s_l2, r_l2, True)

    def along(src, dst, ssem, rsem):
        copies = []
        for k in range(1, NZ):
            zd = (z + k) % NZ
            copies.append(send(src.at[zd], dst.at[k - 1], ssem.at[k - 1], rsem.at[k - 1], at(zz=zd)))
        return copies

    for copy in e2:
        copy.wait_recv()
    ze[0:4] = added(sea[y], ea2, 3).astype(BF16)
    ze[4:8] = added(seb[x], eb2, 3).astype(BF16)
    e3 = along(ze, ze1, s_e3, r_e3)
    for copy in l2:
        copy.wait_recv()
    zl[:, 0:16] = added(sla[y], la2, 3).astype(BF16)
    zl[:, 16:32] = added(slb[x], lb2, 3).astype(BF16)
    l3 = along(zl, zl1, s_l3, r_l3)

    near[2].wait_recv()
    last = jnp.where(tm == NTM - 1, 0.0, part_in[...])
    fg_ref[0:32, :] = part[32:64, :].astype(BF16)
    fg_ref[32:64, :] = (part[64:96, :] + last).astype(BF16)

    def spread(src, dst, ssem, rsem):
        copies = []
        for k in range(1, NTM):
            to = at_tm((tm + k) % NTM)
            copies.append(send(src, dst.at[tm], ssem.at[k - 1], rsem.at[k - 1], to))
        return copies

    for copy in e3:
        copy.wait_recv()
    ge[...] = added(ze[z], ze1, 7) * (1.0 / 256.0)
    ge_in[tm] = ge[...]
    e4 = spread(ge, ge_in, s_e4, r_e4)
    for copy in l3:
        copy.wait_recv()
    gl[...] = added(zl[z], zl1, 7) * (1.0 / 256.0)
    gl_in[tm] = gl[...]
    l4 = spread(gl, gl_in, s_l4, r_l4)
    for copy in e4:
        copy.wait_recv()
    for be in range(8):
        for a in range(3):
            g2_ref[a * 9 + be] = ge_in[be, a * 4 : a * 4 + 4]
    for copy in l4:
        copy.wait_recv()
    for u in range(27):
        tile, row = u // 2, u % 2 * 8
        row += tile % 2 * 16
        g1_ref[u] = gl_in[tile // 2, row : row + 8]
    for a in range(3):
        g2_ref[a * 9 + 8] = gl_in[7, a * 4 : a * 4 + 4]
    for copy in sent:
        copy.wait_send()


def on_device(features, upstream, weight_one, weight_two):
    dma, vmem = pltpu.SemaphoreType.DMA, pltpu.VMEM
    tile = lambda *lead: vmem(lead + (16, 128), BF16)
    pairs = lambda n: [dma((n,)), dma((n,))]
    scratch = [
        vmem((256, 128), BF16), vmem((3, 9, 256, 128), BF16), vmem((3, 9, 128, 128), BF16),
        vmem((256, 576), BF16), vmem((576, 256), BF16), vmem((256, 256), BF16), vmem((512, 384), BF16), dma((8,)),
        vmem((128, 256), BF16), vmem((128, 128), BF16), vmem((256, 128), BF16), vmem((96, 256), BF16),
        vmem((2, 2, 576, 128), BF16), vmem((384, 1152), BF16), vmem((256, 1152), BF16),
        vmem((384, 128), BF16), vmem((384, 128), F32), vmem((128, 1152), BF16), vmem((64, 1152), BF16),
        vmem((256, 256), BF16), vmem((256, 256), BF16), vmem((256, 256), BF16),
        vmem((96, 256), F32), vmem((32, 256), F32),
        tile(NX, NY, 4), tile(NY, NX, 4), tile(NX, NY, 8), tile(NY, NX, 8),
        tile(3, NY, 4), tile(3, NX, 4), tile(3, NY, 8), tile(3, NX, 8),
        tile(NY, 4), tile(NX, 4), tile(NY, 8), tile(NX, 8),
        tile(3, 4), tile(3, 4), tile(3, 8), tile(3, 8),
        vmem((NZ, 16, 128), BF16), vmem((NZ, 32, 128), BF16), vmem((NZ - 1, 16, 128), BF16), vmem((NZ - 1, 32, 128), BF16),
        vmem((16, 128), F32), vmem((32, 128), F32), vmem((NTM, 16, 128), F32), vmem((NTM, 32, 128), F32),
    ]
    scratch += pairs(3) + pairs(4) + pairs(6) * 4 + pairs(7) * 4
    spec = pl.BlockSpec(memory_space=pltpu.VMEM)
    fg, one, two = pl.pallas_call(
        kernel,
        out_shape=(
            jax.ShapeDtypeStruct((64, 256), BF16),
            jax.ShapeDtypeStruct((27, 8, 128), F32),
            jax.ShapeDtypeStruct((27, 4, 128), F32),
        ),
        in_specs=[pl.BlockSpec(memory_space=pltpu.HBM)] * 8,
        out_specs=(spec,) * 3,
        scratch_shapes=scratch,
        compiler_params=pltpu.CompilerParams(
            collective_id=0, has_side_effects=True, vmem_limit_bytes=24 * 1024 * 1024
        ),
    )(
        *(
            pltpu.with_memory_space_constraint(v, pltpu.HBM)
            for v in (
                features.reshape(64, 256),
                upstream.reshape(256, 128),
                weight_one.reshape(3, 9, 256, 128),
                weight_two.reshape(3, 9, 128, 128),
                *tables(),
            )
        )
    )
    return (
        fg.reshape(features.shape),
        one.reshape(3, 3, 3, 8, 128),
        two.reshape(3, 3, 3, 4, 128),
    )


def solution(mesh):
    wide = P("dp", "tm", None, None, None)
    cut = P(None, None, None, "dp", None)
    return jax.shard_map(
        on_device, mesh=mesh, in_specs=(wide, wide, P(), P()), out_specs=(wide, cut, cut), check_vma=False
    )
```

```python
import jax
import jax.numpy as jnp
import numpy as np
from jax import lax
from jax.experimental import pallas as pl
from jax.experimental.pallas import tpu as pltpu
from jax.sharding import PartitionSpec as P

MESH = pl.DeviceIdType.MESH
F32, BF16 = jnp.float32, jnp.bfloat16

NZ, NX, NY, NTM = 8, 4, 4, 8


def tables():
    select = np.zeros((256, 576), np.float32)
    for f in range(4):
        for r in range(4):
            for s in range(16):
                for b in range(3):
                    for e in range(3):
                        rr, ss = r + b - 1, s + e - 1
                        if 0 <= rr < 4 and 0 <= ss < 16:
                            select[f * 64 + r * 16 + s, (b * 3 + e) * 64 + f * 16 + rr // 2 * 8 + ss // 2] = 1
    order_one = np.zeros((256, 256), np.float32)
    order_two = np.zeros((512, 384), np.float32)
    for core in range(2):
        for x_lo in range(2):
            for z in range(8):
                d = (core * 2 + x_lo) * 8 + z
                dp = z * 4 + x_lo * 2 + core
                for k in range(8):
                    order_one[d * 8 + k, dp * 8 + k] = 1
                for a in range(3):
                    for k in range(4):
                        order_two[d * 16 + a * 4 + k, a * 128 + dp * 4 + k] = 1
    return [jnp.asarray(m, BF16) for m in (select, select.T, order_one, order_two)]


def dot(a, b):
    return jnp.dot(a, b, preferred_element_type=F32)


def dot_nt(a, b):
    return lax.dot_general(a, b, (((1,), (1,)), ((), ())), preferred_element_type=F32)


def kernel(
    f_hbm, u_hbm, w1_hbm, w2_hbm, up_hbm, pool_hbm, ord1_hbm, ord2_hbm,
    fg_ref, g1_ref, g2_ref,
    u_ref, w1_ref, w2_ref, up_ref, pool_ref, ord1_ref, ord2_ref, s_in,
    fh, uh, um, uhm, fm, fz, ystk, ycor, u9, u9m, hid, pre_ref, back_ref, slope, p9, p9m, turned, away, away_in, part, part_in,
    ea, eb, la, lb, ea1, eb1, la1, lb1, sea, seb, sla, slb, ea2, eb2, la2, lb2,
    ze, zl, ze1, zl1, ge, gl, ge_in, gl_in,
    s_near, r_near, s_mate, r_mate,
    s_e1, r_e1, s_l1, r_l1, s_e2, r_e2, s_l2, r_l2, s_e3, r_e3, s_l3, r_l3, s_e4, r_e4, s_l4, r_l4,
):
    tm, dp = lax.axis_index("tm"), lax.axis_index("dp")
    y, x_hi = tm // 2, tm % 2
    z, x_lo, core = dp // 4, (dp // 2) % 2, dp % 2
    x = x_lo * 2 + x_hi

    def at(xx=x, yy=y, zz=z, cc=core):
        return {"tm": yy * 2 + xx % 2, "dp": zz * 4 + (xx // 2) * 2 + cc}

    def at_tm(t):
        return {"tm": t, "dp": dp}

    barrier = pltpu.get_barrier_semaphore()
    peers = [at_tm((tm + k) % NTM) for k in range(1, NTM)]
    peers += [at(zz=(z + k) % NZ) for k in range(1, NZ)]
    peers += [at(cc=1 - core)]
    other = (1 - x_lo) * 2
    peers += [at(xx=other), at(xx=other + 1)]
    for peer in peers:
        pl.semaphore_signal(barrier, inc=1, device_id=peer, device_id_type=MESH)

    loads = []
    order = (
        (u_hbm, u_ref), (f_hbm, fh.at[pl.ds(32, 64)]), (w1_hbm, w1_ref), (up_hbm, up_ref),
        (ord2_hbm, ord2_ref), (w2_hbm, w2_ref), (pool_hbm, pool_ref), (ord1_hbm, ord1_ref),
    )
    for i, (src, dst) in enumerate(order):
        loads.append(pltpu.make_async_copy(src, dst, s_in.at[i]))
        loads[i].start()

    sent = []

    def send(src, dst, ssem, rsem, to):
        copy = pltpu.make_async_remote_copy(
            src_ref=src, dst_ref=dst, send_sem=ssem, recv_sem=rsem, device_id=to, device_id_type=MESH
        )
        copy.start()
        sent.append(copy)
        return copy

    def shifted(block, frames, ref, first):
        n = frames * 64
        column = lax.broadcasted_iota(jnp.int32, (n, 128), 0) % 16
        wide = block.astype(F32)
        back_one = jnp.where(column == 15, 0.0, pltpu.roll(wide, n - 1, 0)).astype(BF16)
        on_one = jnp.where(column == 0, 0.0, pltpu.roll(wide, 1, 0)).astype(BF16)
        zero = jnp.zeros((frames, 16, 128), BF16)
        for e, v in enumerate((back_one, block, on_one)):
            v = v.reshape(frames, 64, 128)
            for b in range(3):
                tap = slice((b * 3 + e) * 128, (b * 3 + e + 1) * 128)
                if b == 0:
                    rows = jnp.concatenate([v[:, 16:], zero], axis=1)
                elif b == 1:
                    rows = v
                else:
                    rows = jnp.concatenate([zero, v[:, :48]], axis=1)
                ref[first : first + n, tap] = rows.reshape(n, 128)

    def gate(pre, rows):
        sigma = 1.0 / (1.0 + jnp.exp(-pre))
        hid[128 + rows.start : 128 + rows.stop, :] = (pre * sigma).astype(BF16)
        slope[rows, :] = sigma * (1.0 + pre * (1.0 - sigma))

    def halves(value):
        high = value.astype(BF16)
        return high, (value - high.astype(F32)).astype(BF16)

    def conv_kern(a):
        return jnp.concatenate([w2_ref[a, be] for be in range(9)], axis=1)

    ycor[...] = jnp.zeros(ycor.shape, BF16)
    hid[0:128, :] = jnp.zeros((128, 128), BF16)
    hid[384:512, :] = jnp.zeros((128, 128), BF16)
    u9[256:384, :] = jnp.zeros((128, 1152), BF16)
    p9[0:32, :] = jnp.zeros((32, 1152), BF16)
    p9[96:128, :] = jnp.zeros((32, 1152), BF16)
    loads[0].wait()
    shifted(u_ref[...], 4, u9, 0)
    loads[1].wait()

    pl.semaphore_wait(barrier, len(peers))
    nxt, prv, mate = at_tm((tm + 1) % NTM), at_tm((tm + NTM - 1) % NTM), at(cc=1 - core)
    near = [
        send(fh.at[pl.ds(64, 32)], fh.at[pl.ds(0, 32)], s_near.at[0], r_near.at[0], nxt),
        send(u_ref.at[pl.ds(0, 128)], uh, s_near.at[1], r_near.at[1], prv),
    ]
    from_mate = [
        send(u_ref, um, s_mate.at[0], r_mate.at[0], mate),
        send(fh.at[pl.ds(32, 64)], fm.at[pl.ds(32, 64)], s_mate.at[1], r_mate.at[1], mate),
    ]

    for i in range(2, 4):
        loads[i].wait()
    fz[0:32, :] = jnp.zeros((32, 256), BF16)
    fz[32:96, :] = fh[32:96, :]
    cat = jnp.concatenate([fz[0:64, :], fz[16:80, :], fz[32:96, :]], axis=1)
    for be in range(9):
        rows = slice(be * 64, be * 64 + 64)
        ystk[0, rows, :], ystk[1, rows, :] = halves(dot(cat, w1_ref[:, be].reshape(768, 128)))
    pre = dot(up_ref[...], ystk[0]) + dot(up_ref[...], ystk[1])
    pre_ref[...] = pre[0:128]
    gate(pre[128:256], slice(128, 256))
    for i in range(4, 8):
        loads[i].wait()
    back = jnp.zeros((256, 128), F32)
    for a in range(3):
        back += dot_nt(u9[(2 - a) * 64 : (2 - a) * 64 + 256, :], conv_kern(a))
    back_ref[...] = back
    from_mate[0].wait_recv()
    shifted(um[...], 4, u9m, 0)

    near[0].wait_recv()

    @pl.when(tm == 0)
    def _():
        fh[0:32, :] = jnp.zeros((32, 256), BF16)

    from_mate.append(send(fh.at[pl.ds(0, 32)], fm.at[pl.ds(0, 32)], s_mate.at[2], r_mate.at[2], mate))
    one = jnp.concatenate([fh[0:16, :], fh[16:32, :]], axis=1)
    two = jnp.concatenate([fh[16:32, :], jnp.zeros((16, 256), BF16)], axis=1)
    cat = jnp.concatenate([one, two], axis=0)
    for be in range(9):
        rows = slice(be * 64, be * 64 + 32)
        ycor[0, rows, :], ycor[1, rows, :] = halves(dot(cat, w1_ref[0:2, be].reshape(512, 128)))
    gate(pre_ref[...] + (dot(up_ref[0:128, :], ycor[0]) + dot(up_ref[0:128, :], ycor[1])), slice(0, 128))

    taps = jnp.concatenate([hid[a * 64 : a * 64 + 384, :] for a in range(3)], axis=1)
    away[...] = dot_nt(ord2_ref[pl.ds(pl.multiple_of((1 - core) * 256, 256), 256), :], taps).astype(BF16)
    from_mate.append(send(away, away_in, s_mate.at[3], r_mate.at[3], mate))

    near[1].wait_recv()

    @pl.when(tm == NTM - 1)
    def _():
        uh[...] = jnp.zeros((128, 128), BF16)

    from_mate.append(send(uh, uhm, s_mate.at[4], r_mate.at[4], mate))
    shifted(uh[...], 2, u9, 256)
    later = dot_nt(u9[256:384, :], conv_kern(0))
    third = jnp.concatenate([jnp.zeros((64, 1152), BF16), u9[256:320, :]], axis=0)
    later += dot_nt(third, conv_kern(1))
    back_ref[128:256, :] += later
    dpre = (back_ref[...] * slope[...]).astype(BF16)
    pooled = dot(pool_ref[...], dpre).astype(BF16)
    for be in range(9):
        p9[32:96, be * 128 : be * 128 + 128] = pooled[be * 64 : be * 64 + 64]
    from_mate.append(send(p9.at[pl.ds(32, 64)], p9m, s_mate.at[5], r_mate.at[5], mate))
    turned[...] = dot_nt(ord2_ref[pl.ds(pl.multiple_of(core * 256, 256), 256), :], taps).astype(BF16)

    def put_late(tile, value):
        value = value.reshape(2, 8, 16, 128)
        for lo in range(2):
            xx, yy = lo * 2 + tile // 2 % 2, tile // 4
            if tile % 2 == 0:
                la[xx, yy] = value[lo]
            else:
                lb[yy, xx] = value[lo]

    from_mate[4].wait_recv()
    shifted(uhm[...], 2, u9m, 256)
    from_mate[3].wait_recv()
    for be in range(9):
        tap = slice(be * 128, be * 128 + 128)
        two = dot(turned[...], u9[:, tap]) + dot(away_in[...], u9m[:, tap])
        two = two.astype(BF16)
        if be == 8:
            put_late(14, two)
        else:
            two = two.reshape(2, 8, 16, 128)
            for lo in range(2):
                xx, yy = lo * 2 + be % 2, be // 2
                ea[xx, yy] = two[lo, :4]
                eb[yy, xx] = two[lo, 4:]

    def around(src_a, src_b, dst_a, dst_b, ssem, rsem, swap):
        copies = []
        for k in range(1, 4):
            xd, yd = (x + k) % NX, (y + k) % NY
            ia, ib = (yd, xd) if swap else (xd, yd)
            to_a, to_b = (at(yy=yd), at(xx=xd)) if swap else (at(xx=xd), at(yy=yd))
            copies.append(send(src_a.at[ia], dst_a.at[k - 1], ssem.at[2 * k - 2], rsem.at[2 * k - 2], to_a))
            copies.append(send(src_b.at[ib], dst_b.at[k - 1], ssem.at[2 * k - 1], rsem.at[2 * k - 1], to_b))
        return copies

    def added(own, parts, count):
        total = own.astype(F32)
        for k in range(count):
            total += parts[k].astype(F32)
        return total

    e1 = around(ea, eb, ea1, eb1, s_e1, r_e1, False)

    from_mate[1].wait_recv()
    from_mate[2].wait_recv()
    feats = []
    mine = pl.ds(pl.multiple_of(core * 128, 128), 128)
    for a in range(3):
        rows = jnp.concatenate([fh[a * 16 : a * 16 + 64, :], fm[a * 16 : a * 16 + 64, :]], axis=0)
        feats.append(dot_nt(ord1_ref[mine, :], rows).astype(BF16))
    from_mate[5].wait_recv()
    units = []
    pools = jnp.concatenate([p9[32:96, :], p9m[...]], axis=0)
    for a in range(3):
        for be in range(9):
            units.append(dot(feats[a], pools[:, be * 128 : be * 128 + 128]).reshape(16, 8, 128))
            if len(units) == 2:
                put_late((a * 9 + be) // 2, jnp.concatenate(units, axis=1).astype(BF16))
                units = []
    units.append(jnp.zeros((16, 8, 128), F32))
    put_late(13, jnp.concatenate(units, axis=1).astype(BF16))
    put_late(15, jnp.zeros((16, 16, 128), BF16))
    l1 = around(la, lb, la1, lb1, s_l1, r_l1, False)
    result = jnp.zeros((96, 256), F32)
    for a in range(3):
        kern = jnp.concatenate([w1_ref[a, be] for be in range(9)], axis=1)
        result += dot_nt(p9[(2 - a) * 16 : (2 - a) * 16 + 96, :], kern)
    part[...] = result
    near.append(send(part.at[pl.ds(0, 32)], part_in, s_near.at[2], r_near.at[2], prv))

    for copy in e1:
        copy.wait_recv()
    sea[...] = added(ea[x], ea1, 3).astype(BF16)
    seb[...] = added(eb[y], eb1, 3).astype(BF16)
    e2 = around(sea, seb, ea2, eb2, s_e2, r_e2, True)
    for copy in l1:
        copy.wait_recv()
    sla[...] = added(la[x], la1, 3).astype(BF16)
    slb[...] = added(lb[y], lb1, 3).astype(BF16)
    l2 = around(sla, slb, la2, lb2, s_l2, r_l2, True)

    def along(src, dst, ssem, rsem):
        copies = []
        for k in range(1, NZ):
            zd = (z + k) % NZ
            copies.append(send(src.at[zd], dst.at[k - 1], ssem.at[k - 1], rsem.at[k - 1], at(zz=zd)))
        return copies

    for copy in e2:
        copy.wait_recv()
    ze[0:4] = added(sea[y], ea2, 3).astype(BF16)
    ze[4:8] = added(seb[x], eb2, 3).astype(BF16)
    e3 = along(ze, ze1, s_e3, r_e3)
    for copy in l2:
        copy.wait_recv()
    zl[:, 0:16] = added(sla[y], la2, 3).astype(BF16)
    zl[:, 16:32] = added(slb[x], lb2, 3).astype(BF16)
    l3 = along(zl, zl1, s_l3, r_l3)

    near[2].wait_recv()
    last = jnp.where(tm == NTM - 1, 0.0, part_in[...])
    fg_ref[0:32, :] = part[32:64, :].astype(BF16)
    fg_ref[32:64, :] = (part[64:96, :] + last).astype(BF16)

    def spread(src, dst, ssem, rsem):
        copies = []
        for k in range(1, NTM):
            to = at_tm((tm + k) % NTM)
            copies.append(send(src, dst.at[tm], ssem.at[k - 1], rsem.at[k - 1], to))
        return copies

    for copy in e3:
        copy.wait_recv()
    ge[...] = added(ze[z], ze1, 7).astype(BF16)
    ge_in[tm] = ge[...]
    e4 = spread(ge, ge_in, s_e4, r_e4)
    for copy in l3:
        copy.wait_recv()
    gl[...] = added(zl[z], zl1, 7).astype(BF16)
    gl_in[tm] = gl[...]
    l4 = spread(gl, gl_in, s_l4, r_l4)
    for copy in e4:
        copy.wait_recv()
    factor = 1.0 / 256.0
    for be in range(8):
        rows = ge_in[be].astype(F32) * factor
        for a in range(3):
            g2_ref[a * 9 + be] = rows[a * 4 : a * 4 + 4]
    for copy in l4:
        copy.wait_recv()
    for tile in range(15):
        rows = gl_in[tile // 2, tile % 2 * 16 : tile % 2 * 16 + 16, :].astype(F32) * factor
        if tile < 14:
            g1_ref[2 * tile] = rows[0:8]
        if tile < 13:
            g1_ref[2 * tile + 1] = rows[8:16]
        if tile == 14:
            for a in range(3):
                g2_ref[a * 9 + 8] = rows[a * 4 : a * 4 + 4]
    for copy in sent:
        copy.wait_send()


def store(*refs):
    sems = refs[6]
    copies = [pltpu.make_async_copy(refs[i], refs[3 + i], sems.at[i]) for i in range(3)]
    for copy in copies:
        copy.start()
    for copy in copies:
        copy.wait()


def on_device(features, upstream, weight_one, weight_two):
    dma, vmem = pltpu.SemaphoreType.DMA, pltpu.VMEM
    tile = lambda *lead: vmem(lead + (16, 128), BF16)
    pairs = lambda n: [dma((n,)), dma((n,))]
    scratch = [
        vmem((256, 128), BF16), vmem((3, 9, 256, 128), BF16), vmem((3, 9, 128, 128), BF16),
        vmem((256, 576), BF16), vmem((576, 256), BF16), vmem((256, 256), BF16), vmem((512, 384), BF16), dma((8,)),
        vmem((96, 256), BF16), vmem((128, 128), BF16), vmem((256, 128), BF16), vmem((128, 128), BF16),
        vmem((96, 256), BF16), vmem((96, 256), BF16),
        vmem((2, 576, 128), BF16), vmem((2, 576, 128), BF16), vmem((384, 1152), BF16), vmem((384, 1152), BF16),
        vmem((512, 128), BF16), vmem((128, 128), F32), vmem((256, 128), F32), vmem((256, 128), F32),
        vmem((128, 1152), BF16), vmem((64, 1152), BF16),
        vmem((256, 384), BF16), vmem((256, 384), BF16), vmem((256, 384), BF16),
        vmem((96, 256), F32), vmem((32, 256), F32),
        tile(NX, NY, 4), tile(NY, NX, 4), tile(NX, NY, 8), tile(NY, NX, 8),
        tile(3, NY, 4), tile(3, NX, 4), tile(3, NY, 8), tile(3, NX, 8),
        tile(NY, 4), tile(NX, 4), tile(NY, 8), tile(NX, 8),
        tile(3, 4), tile(3, 4), tile(3, 8), tile(3, 8),
        vmem((NZ, 16, 128), BF16), vmem((NZ, 32, 128), BF16), vmem((NZ - 1, 16, 128), BF16), vmem((NZ - 1, 32, 128), BF16),
        vmem((16, 128), BF16), vmem((32, 128), BF16), vmem((NTM, 16, 128), BF16), vmem((NTM, 32, 128), BF16),
    ]
    scratch += pairs(3) + pairs(6) + pairs(6) * 4 + pairs(7) * 4
    spec = pl.BlockSpec(memory_space=pltpu.VMEM)
    shapes = (
        jax.ShapeDtypeStruct((64, 256), BF16),
        jax.ShapeDtypeStruct((27, 8, 128), F32),
        jax.ShapeDtypeStruct((27, 4, 128), F32),
    )
    results = pl.pallas_call(
        kernel,
        out_shape=shapes,
        in_specs=[pl.BlockSpec(memory_space=pltpu.HBM)] * 8,
        out_specs=(spec,) * 3,
        scratch_shapes=scratch,
        compiler_params=pltpu.CompilerParams(
            collective_id=0, has_side_effects=True, vmem_limit_bytes=24 * 1024 * 1024
        ),
    )(
        *(
            pltpu.with_memory_space_constraint(v, pltpu.HBM)
            for v in (
                features.reshape(64, 256),
                upstream.reshape(256, 128),
                weight_one.reshape(3, 9, 256, 128),
                weight_two.reshape(3, 9, 128, 128),
                *tables(),
            )
        )
    )
    fg, one, two = pl.pallas_call(
        store,
        out_shape=shapes,
        in_specs=[spec] * 3,
        out_specs=(pl.BlockSpec(memory_space=pltpu.HBM),) * 3,
        scratch_shapes=[dma((3,))],
    )(*(pltpu.with_memory_space_constraint(v, pltpu.VMEM) for v in results))
    return (
        fg.reshape(features.shape),
        one.reshape(3, 3, 3, 8, 128),
        two.reshape(3, 3, 3, 4, 128),
    )


def solution(mesh):
    wide = P("dp", "tm", None, None, None)
    cut = P(None, None, None, "dp", None)
    return jax.shard_map(
        on_device, mesh=mesh, in_specs=(wide, wide, P(), P()), out_specs=(wide, cut, cut), check_vma=False
    )
```

```python
import jax
import jax.numpy as jnp
import numpy as np
from jax import lax
from jax.experimental import pallas as pl
from jax.experimental.pallas import tpu as pltpu
from jax.sharding import PartitionSpec as P

MESH = pl.DeviceIdType.MESH
F32, BF16 = jnp.float32, jnp.bfloat16

NZ, NX, NY, NTM = 8, 4, 4, 8
CUT = 5


def tables():
    select = np.zeros((256, 576), np.float32)
    for f in range(4):
        for r in range(4):
            for s in range(16):
                for b in range(3):
                    for e in range(3):
                        rr, ss = r + b - 1, s + e - 1
                        if 0 <= rr < 4 and 0 <= ss < 16:
                            select[f * 64 + r * 16 + s, (b * 3 + e) * 64 + f * 16 + rr // 2 * 8 + ss // 2] = 1
    order_one = np.zeros((256, 256), np.float32)
    order_two = np.zeros((512, 384), np.float32)
    for core in range(2):
        for x_lo in range(2):
            for z in range(8):
                d = (core * 2 + x_lo) * 8 + z
                dp = z * 4 + x_lo * 2 + core
                for k in range(8):
                    order_one[d * 8 + k, dp * 8 + k] = 1
                for a in range(3):
                    for k in range(4):
                        order_two[d * 16 + a * 4 + k, a * 128 + dp * 4 + k] = 1
    return [jnp.asarray(m, BF16) for m in (select, select.T, order_one, order_two)]


def dot(a, b):
    return jnp.dot(a, b, preferred_element_type=F32)


def dot_nt(a, b):
    return lax.dot_general(a, b, (((1,), (1,)), ((), ())), preferred_element_type=F32)


def kernel(
    f_hbm, u_hbm, w1_hbm, w2_hbm, up_hbm, pool_hbm, ord1_hbm, ord2_hbm,
    fg_ref, g1_ref, g2_ref,
    u_ref, w1_ref, w2_ref, up_ref, pool_ref, ord1_ref, ord2_ref, s_in,
    fh, uh, um, uhm, fm, fz, ystk, ycor, u9, u9m, hid, pre_ref, back_ref, slope, p9, p9m, turned, away, away_in, part, part_in,
    sum_a, sum_b, in_a, in_b, mid_a, mid_b, mid_in_a, mid_in_b, last, last_in, own, gath,
    final, c_sum, c_in, c_mid, c_mid_in, c_end, c_end_in, d_sum, d_in, d_mid, d_mid_in, d_end, d_end_in,
    s_near, r_near, s_mate, r_mate, s_one, r_one, s_two, r_two, s_three, r_three, s_four, r_four,
    s_c1, r_c1, s_c2, r_c2, s_c3, r_c3, s_d1, r_d1, s_d2, r_d2, s_d3, r_d3,
):
    tm, dp = lax.axis_index("tm"), lax.axis_index("dp")
    y, x_hi = tm // 2, tm % 2
    z, x_lo, core = dp // 4, (dp // 2) % 2, dp % 2
    x = x_lo * 2 + x_hi

    def at(xx=x, yy=y, zz=z, cc=core):
        return {"tm": yy * 2 + xx % 2, "dp": zz * 4 + (xx // 2) * 2 + cc}

    def at_tm(t):
        return {"tm": t, "dp": dp}

    barrier = pltpu.get_barrier_semaphore()
    peers = [at_tm((tm + k) % NTM) for k in range(1, NTM)]
    peers += [at(zz=(z + k) % NZ) for k in range(1, NZ)]
    peers += [at(cc=1 - core)]
    other = (1 - x_lo) * 2
    peers += [at(xx=other), at(xx=other + 1)]
    for peer in peers:
        pl.semaphore_signal(barrier, inc=1, device_id=peer, device_id_type=MESH)

    loads = []
    order = (
        (u_hbm, u_ref), (f_hbm, fh.at[pl.ds(32, 64)]), (up_hbm, up_ref),
        (ord2_hbm, ord2_ref), (pool_hbm, pool_ref), (ord1_hbm, ord1_ref),
    )
    for i, (src, dst) in enumerate(order):
        loads.append(pltpu.make_async_copy(src, dst, s_in.at[i]))
    one, two = [], []
    for be in range(9):
        tap = pl.ds(be * 128, 128)
        one.append(pltpu.make_async_copy(w1_hbm.at[:, be], w1_ref.at[:, :, tap], s_in.at[6 + be]))
        two.append(pltpu.make_async_copy(w2_hbm.at[:, be], w2_ref.at[:, :, tap], s_in.at[15 + be]))
    for copy in loads[:2] + one + loads[2:3] + two + loads[3:]:
        copy.start()

    sent = []

    def send(src, dst, ssem, rsem, to):
        copy = pltpu.make_async_remote_copy(
            src_ref=src, dst_ref=dst, send_sem=ssem, recv_sem=rsem, device_id=to, device_id_type=MESH
        )
        copy.start()
        sent.append(copy)
        return copy

    def shifted(block, frames, ref, first):
        n = frames * 64
        column = lax.broadcasted_iota(jnp.int32, (n, 128), 0) % 16
        wide = block.astype(F32)
        back_one = jnp.where(column == 15, 0.0, pltpu.roll(wide, n - 1, 0)).astype(BF16)
        on_one = jnp.where(column == 0, 0.0, pltpu.roll(wide, 1, 0)).astype(BF16)
        zero = jnp.zeros((frames, 16, 128), BF16)
        for e, v in enumerate((back_one, block, on_one)):
            v = v.reshape(frames, 64, 128)
            for b in range(3):
                tap = slice((b * 3 + e) * 128, (b * 3 + e + 1) * 128)
                if b == 0:
                    rows = jnp.concatenate([v[:, 16:], zero], axis=1)
                elif b == 1:
                    rows = v
                else:
                    rows = jnp.concatenate([zero, v[:, :48]], axis=1)
                ref[first : first + n, tap] = rows.reshape(n, 128)

    def gate(pre, rows):
        sigma = 1.0 / (1.0 + jnp.exp(-pre))
        hid[128 + rows.start : 128 + rows.stop, :] = (pre * sigma).astype(BF16)
        slope[rows, :] = sigma * (1.0 + pre * (1.0 - sigma))

    def halves(value):
        high = value.astype(BF16)
        return high, (value - high.astype(F32)).astype(BF16)

    def keep_halves(value, ref):
        high, low = halves(value)
        n = value.shape[0]
        for be in range(9):
            tap, rows = slice(be * 128, be * 128 + 128), slice(be * 64, be * 64 + n)
            ref[rows, 0:128] = high[:, tap]
            ref[rows, 128:256] = low[:, tap]

    def widened(rows, ref):
        both = dot(up_ref[0:rows, :], ref[...])
        return both[:, 0:128] + both[:, 128:256]

    ycor[...] = jnp.zeros(ycor.shape, BF16)
    hid[0:128, :] = jnp.zeros((128, 128), BF16)
    hid[384:512, :] = jnp.zeros((128, 128), BF16)
    u9[256:384, :] = jnp.zeros((128, 1152), BF16)
    p9[0:32, :] = jnp.zeros((32, 1152), BF16)
    p9[96:128, :] = jnp.zeros((32, 1152), BF16)
    loads[0].wait()
    shifted(u_ref[...], 4, u9, 0)
    loads[1].wait()

    pl.semaphore_wait(barrier, len(peers))
    nxt, prv, mate = at_tm((tm + 1) % NTM), at_tm((tm + NTM - 1) % NTM), at(cc=1 - core)
    near = [
        send(fh.at[pl.ds(64, 32)], fh.at[pl.ds(0, 32)], s_near.at[0], r_near.at[0], nxt),
        send(u_ref.at[pl.ds(0, 128)], uh, s_near.at[1], r_near.at[1], prv),
    ]
    from_mate = [
        send(u_ref, um, s_mate.at[0], r_mate.at[0], mate),
        send(fh.at[pl.ds(32, 64)], fm.at[pl.ds(32, 64)], s_mate.at[1], r_mate.at[1], mate),
    ]

    for copy in one + loads[2:3]:
        copy.wait()
    fz[0:32, :] = jnp.zeros((32, 256), BF16)
    fz[32:96, :] = fh[32:96, :]
    cat = jnp.concatenate([fz[0:64, :], fz[16:80, :], fz[32:96, :]], axis=1)
    keep_halves(dot(cat, w1_ref[...].reshape(768, 1152)), ystk)
    pre = widened(256, ystk)
    pre_ref[...] = pre[0:128]
    gate(pre[128:256], slice(128, 256))
    for copy in two + loads[3:]:
        copy.wait()
    back = jnp.zeros((256, 128), F32)
    for a in range(3):
        back += dot_nt(u9[(2 - a) * 64 : (2 - a) * 64 + 256, :], w2_ref[a])
    back_ref[...] = back
    from_mate[0].wait_recv()
    shifted(um[...], 4, u9m, 0)

    near[0].wait_recv()

    @pl.when(tm == 0)
    def _():
        fh[0:32, :] = jnp.zeros((32, 256), BF16)

    from_mate.append(send(fh.at[pl.ds(0, 32)], fm.at[pl.ds(0, 32)], s_mate.at[2], r_mate.at[2], mate))
    head = jnp.concatenate([fh[0:16, :], fh[16:32, :]], axis=1)
    tail = jnp.concatenate([fh[16:32, :], jnp.zeros((16, 256), BF16)], axis=1)
    cat = jnp.concatenate([head, tail], axis=0)
    keep_halves(dot(cat, w1_ref[0:2].reshape(512, 1152)), ycor)
    gate(pre_ref[...] + widened(128, ycor), slice(0, 128))

    taps = jnp.concatenate([hid[a * 64 : a * 64 + 384, :] for a in range(3)], axis=1)
    away[...] = dot_nt(ord2_ref[pl.ds(pl.multiple_of((1 - core) * 256, 256), 256), :], taps).astype(BF16)
    from_mate.append(send(away, away_in, s_mate.at[3], r_mate.at[3], mate))

    near[1].wait_recv()

    @pl.when(tm == NTM - 1)
    def _():
        uh[...] = jnp.zeros((128, 128), BF16)

    from_mate.append(send(uh, uhm, s_mate.at[4], r_mate.at[4], mate))
    shifted(uh[...], 2, u9, 256)
    later = dot_nt(u9[256:384, :], w2_ref[0:2].reshape(256, 1152))
    back_ref[128:256, :] += later[:, 0:128]
    back_ref[192:256, :] += later[0:64, 128:256]
    dpre = (back_ref[...] * slope[...]).astype(BF16)
    pooled = dot(pool_ref[...], dpre).astype(BF16)
    for be in range(9):
        p9[32:96, be * 128 : be * 128 + 128] = pooled[be * 64 : be * 64 + 64]
    from_mate.append(send(p9.at[pl.ds(32, 64)], p9m, s_mate.at[5], r_mate.at[5], mate))
    turned[...] = dot_nt(ord2_ref[pl.ds(pl.multiple_of(core * 256, 256), 256), :], taps).astype(BF16)

    def put(chain, j, value):
        value = value.reshape(2, 8, 16, 128)
        for lo in range(2):
            sum_a[chain, lo * 2 + j % 2, j // 2] = value[lo, :CUT]
            sum_b[chain, j // 2, lo * 2 + j % 2] = value[lo, CUT:]

    def put_two(j, value):
        value = value.reshape(2, 8, 16, 128)
        for zz in range(NZ):
            c_sum[zz, j // 2, j % 2] = value[0, zz]
        d_sum[j // 2, j % 2] = value[1]

    from_mate[4].wait_recv()
    shifted(uhm[...], 2, u9m, 256)
    from_mate[3].wait_recv()
    for first in range(0, 9, 2):
        tap = slice(first * 128, min(first * 128 + 256, 1152))
        pair = dot(turned[...], u9[:, tap]) + dot(away_in[...], u9m[:, tap])
        pair = pair.astype(BF16)
        if first == 8:
            put(1, 6, pair)
        else:
            put_two(first, pair[:, 0:128])
            put_two(first + 1, pair[:, 128:256])

    def around(chain, swap):
        copies = []
        src_a, src_b, dst_a, dst_b = (mid_a, mid_b, mid_in_a, mid_in_b) if swap else (sum_a, sum_b, in_a, in_b)
        ssem, rsem = (s_two, r_two) if swap else (s_one, r_one)
        for k in range(1, 4):
            xd, yd = (x + k) % NX, (y + k) % NY
            ia, ib = (yd, xd) if swap else (xd, yd)
            to_a, to_b = (at(yy=yd), at(xx=xd)) if swap else (at(xx=xd), at(yy=yd))
            for src, dst, index, to, n in ((src_a, dst_a, ia, to_a, 2 * k - 2), (src_b, dst_b, ib, to_b, 2 * k - 1)):
                copies.append(send(src.at[chain, index], dst.at[chain, k - 1], ssem.at[chain, n], rsem.at[chain, n], to))
        return copies

    def landed(copies):
        for copy in copies:
            copy.wait_recv()

    def added(own, parts, count):
        total = own.astype(F32)
        for k in range(count):
            total += parts[k].astype(F32)
        return total.astype(BF16)

    def stage_two(chain, copies):
        landed(copies)
        mid_a[chain] = added(sum_a[chain, x], in_a.at[chain], 3)
        mid_b[chain] = added(sum_b[chain, y], in_b.at[chain], 3)
        return around(chain, True)

    def stage_three(chain, copies):
        landed(copies)
        last[chain, 0:CUT] = added(mid_a[chain, y], mid_in_a.at[chain], 3)
        last[chain, CUT:NZ] = added(mid_b[chain, x], mid_in_b.at[chain], 3)
        copies = []
        for k in range(1, NZ):
            zd = (z + k) % NZ
            copies.append(send(
                last.at[chain, zd], last_in.at[chain, k - 1], s_three.at[chain, k - 1], r_three.at[chain, k - 1], at(zz=zd)
            ))
        return copies

    def stage_four(chain, total):
        own[chain] = total
        gath[chain, tm] = total
        copies = []
        for k in range(1, NTM):
            to = at_tm((tm + k) % NTM)
            copies.append(send(own.at[chain], gath.at[chain, tm], s_four.at[chain, k - 1], r_four.at[chain, k - 1], to))
        return copies

    def within(src, dst, ssem, rsem, lo):
        def copy(slot, index, to_hi):
            return pltpu.make_async_remote_copy(
                src_ref=src.at[index], dst_ref=dst.at[slot], send_sem=ssem.at[slot], recv_sem=rsem.at[slot],
                device_id=at(xx=lo * 2 + to_hi), device_id_type=MESH,
            )

        home = (copy(0, 1 - x_hi, 1 - x_hi),)
        abroad = (copy(1, x_hi, x_hi), copy(2, 1 - x_hi, 1 - x_hi))
        return home, abroad

    def each(condition, copies, method):
        @pl.when(condition)
        def _():
            for copy in copies:
                getattr(copy, method)()

    def over_y(src, dst, ssem, rsem):
        copies = []
        for k in range(1, NY):
            yd = (y + k) % NY
            copies.append(send(src.at[yd], dst.at[k - 1], ssem.at[k - 1], rsem.at[k - 1], at(yy=yd)))
        return copies

    c1 = []
    for k in range(1, NZ):
        zd = (z + k) % NZ
        c1.append(send(c_sum.at[zd], c_in.at[k - 1], s_c1.at[k - 1], r_c1.at[k - 1], at(zz=zd)))
    d1 = over_y(d_sum, d_in, s_d1, r_d1)

    from_mate[1].wait_recv()
    from_mate[2].wait_recv()
    feats = []
    mine = pl.ds(pl.multiple_of(core * 128, 128), 128)
    for a in range(3):
        rows = jnp.concatenate([fh[a * 16 : a * 16 + 64, :], fm[a * 16 : a * 16 + 64, :]], axis=0)
        feats.append(dot_nt(ord1_ref[mine, :], rows).astype(BF16))
    from_mate[5].wait_recv()
    units = []
    pools = jnp.concatenate([p9[32:96, :], p9m[...]], axis=0)
    for a in range(3):
        whole = dot(feats[a], pools)
        for be in range(9):
            units.append(whole[:, be * 128 : be * 128 + 128].reshape(16, 8, 128))
            if len(units) == 2:
                tile = (a * 9 + be) // 2
                put(tile // 8, tile % 8, jnp.concatenate(units, axis=1).astype(BF16))
                units = []
    units.append(jnp.zeros((16, 8, 128), F32))
    put(1, 5, jnp.concatenate(units, axis=1).astype(BF16))
    put(1, 7, jnp.zeros((16, 16, 128), BF16))
    f1 = around(0, False)
    l1 = around(1, False)

    result = jnp.zeros((96, 256), F32)
    for a in range(3):
        result += dot_nt(p9[(2 - a) * 16 : (2 - a) * 16 + 96, :], w1_ref[a])
    part[...] = result
    near.append(send(part.at[pl.ds(0, 32)], part_in, s_near.at[2], r_near.at[2], prv))

    landed(d1)
    d_mid[...] = added(d_sum[y], d_in, 3)
    d_home, d_abroad = within(d_mid, d_mid_in, s_d2, r_d2, 1)
    each(x_lo == 1, d_home, "start")
    each(x_lo == 0, d_abroad, "start")
    f2 = stage_two(0, f1)
    l2 = stage_two(1, l1)
    landed(c1)
    c_mid[...] = added(c_sum[z], c_in, 7)
    c2 = over_y(c_mid, c_mid_in, s_c2, r_c2)
    f3 = stage_three(0, f2)

    d3 = []
    for k in range(1, NZ):
        zd = (z + k) % NZ
        d3.append(pltpu.make_async_remote_copy(
            src_ref=d_end.at[zd], dst_ref=d_end_in.at[k - 1], send_sem=s_d3.at[k - 1], recv_sem=r_d3.at[k - 1],
            device_id=at(zz=zd), device_id_type=MESH,
        ))

    @pl.when(x_lo == 1)
    def _():
        for copy in d_home + d_abroad:
            copy.wait_recv()
        d_end[...] = added(d_mid[x_hi], d_mid_in, 3)
        for copy in d3:
            copy.start()

    l3 = stage_three(1, l2)
    landed(c2)
    c_end[...] = added(c_mid[y], c_mid_in, 3)
    c_home, c_abroad = within(c_end, c_end_in, s_c3, r_c3, 0)
    each(x_lo == 0, c_home, "start")
    each(x_lo == 1, c_abroad, "start")
    near[2].wait_recv()
    added_late = jnp.where(tm == NTM - 1, 0.0, part_in[...])
    fg_ref[0:32, :] = part[32:64, :].astype(BF16)
    fg_ref[32:64, :] = (part[64:96, :] + added_late).astype(BF16)
    landed(f3)
    f4 = stage_four(0, added(last[0, z], last_in.at[0], 7))

    @pl.when(x_lo == 0)
    def _():
        for copy in c_home + c_abroad:
            copy.wait_recv()
        final[...] = added(c_end[x_hi], c_end_in, 3)

    @pl.when(x_lo == 1)
    def _():
        for copy in d3:
            copy.wait_recv()
        final[...] = added(d_end[z], d_end_in, 7)

    e4 = stage_four(2, final[...])
    landed(l3)
    l4 = stage_four(1, added(last[1, z], last_in.at[1], 7))

    factor = 1.0 / 256.0
    landed(e4)
    for be in range(8):
        rows = gath[2, be].astype(F32) * factor
        for a in range(3):
            g2_ref[a * 9 + be] = rows[a * 4 : a * 4 + 4]
    landed(f4)
    for tile in range(15):
        if tile == 8:
            landed(l4)
        rows = gath[tile // 8, tile % 8].astype(F32) * factor
        if tile < 14:
            g1_ref[2 * tile] = rows[0:8]
        if tile < 13:
            g1_ref[2 * tile + 1] = rows[8:16]
        if tile == 14:
            for a in range(3):
                g2_ref[a * 9 + 8] = rows[a * 4 : a * 4 + 4]
    each(x_lo == 1, d_home + tuple(d3) + c_abroad, "wait_send")
    each(x_lo == 0, d_abroad + c_home, "wait_send")
    for copy in sent:
        copy.wait_send()


def store(*refs):
    sems = refs[6]
    copies = [pltpu.make_async_copy(refs[i], refs[3 + i], sems.at[i]) for i in range(3)]
    for copy in copies:
        copy.start()
    for copy in copies:
        copy.wait()


def on_device(features, upstream, weight_one, weight_two):
    dma, vmem = pltpu.SemaphoreType.DMA, pltpu.VMEM
    tile = lambda *lead: vmem(lead + (16, 128), BF16)
    pairs = lambda shape: [dma(shape), dma(shape)]
    scratch = [
        vmem((256, 128), BF16), vmem((3, 256, 1152), BF16), vmem((3, 128, 1152), BF16),
        vmem((256, 576), BF16), vmem((576, 256), BF16), vmem((256, 256), BF16), vmem((512, 384), BF16), dma((24,)),
        vmem((96, 256), BF16), vmem((128, 128), BF16), vmem((256, 128), BF16), vmem((128, 128), BF16),
        vmem((96, 256), BF16), vmem((96, 256), BF16),
        vmem((576, 256), BF16), vmem((576, 256), BF16), vmem((384, 1152), BF16), vmem((384, 1152), BF16),
        vmem((512, 128), BF16), vmem((128, 128), F32), vmem((256, 128), F32), vmem((256, 128), F32),
        vmem((128, 1152), BF16), vmem((64, 1152), BF16),
        vmem((256, 384), BF16), vmem((256, 384), BF16), vmem((256, 384), BF16),
        vmem((96, 256), F32), vmem((32, 256), F32),
        tile(2, NX, NY, CUT), tile(2, NY, NX, NZ - CUT), tile(2, 3, NY, CUT), tile(2, 3, NX, NZ - CUT),
        tile(2, NY, CUT), tile(2, NX, NZ - CUT), tile(2, 3, CUT), tile(2, 3, NZ - CUT),
        tile(2, NZ), tile(2, NZ - 1), tile(3), tile(3, NTM),
        tile(), tile(NZ, NY, 2), tile(NZ - 1, NY, 2), tile(NY, 2), tile(3, 2), tile(2), tile(3),
        tile(NY, 2, NZ), tile(3, 2, NZ), tile(2, NZ), tile(3, NZ), tile(NZ), tile(NZ - 1),
    ]
    scratch += pairs((3,)) + pairs((6,)) + pairs((2, 6)) * 2 + pairs((2, 7)) + pairs((3, 7))
    scratch += pairs((7,)) + pairs((3,)) * 4 + pairs((7,))
    spec = pl.BlockSpec(memory_space=pltpu.VMEM)
    shapes = (
        jax.ShapeDtypeStruct((64, 256), BF16),
        jax.ShapeDtypeStruct((27, 8, 128), F32),
        jax.ShapeDtypeStruct((27, 4, 128), F32),
    )
    results = pl.pallas_call(
        kernel,
        out_shape=shapes,
        in_specs=[pl.BlockSpec(memory_space=pltpu.HBM)] * 8,
        out_specs=(spec,) * 3,
        scratch_shapes=scratch,
        compiler_params=pltpu.CompilerParams(
            collective_id=0, has_side_effects=True, vmem_limit_bytes=24 * 1024 * 1024
        ),
    )(
        *(
            pltpu.with_memory_space_constraint(v, pltpu.HBM)
            for v in (
                features.reshape(64, 256),
                upstream.reshape(256, 128),
                weight_one.reshape(3, 9, 256, 128),
                weight_two.reshape(3, 9, 128, 128),
                *tables(),
            )
        )
    )
    fg, one, two = pl.pallas_call(
        store,
        out_shape=shapes,
        in_specs=[spec] * 3,
        out_specs=(pl.BlockSpec(memory_space=pltpu.HBM),) * 3,
        scratch_shapes=[dma((3,))],
    )(*(pltpu.with_memory_space_constraint(v, pltpu.VMEM) for v in results))
    return (
        fg.reshape(features.shape),
        one.reshape(3, 3, 3, 8, 128),
        two.reshape(3, 3, 3, 4, 128),
    )


def solution(mesh):
    wide = P("dp", "tm", None, None, None)
    cut = P(None, None, None, "dp", None)
    return jax.shard_map(
        on_device, mesh=mesh, in_specs=(wide, wide, P(), P()), out_specs=(wide, cut, cut), check_vma=False
    )
```

```python
import jax
import jax.numpy as jnp
import numpy as np
from jax import lax
from jax.experimental import pallas as pl
from jax.experimental.pallas import tpu as pltpu
from jax.sharding import PartitionSpec as P

MESH = pl.DeviceIdType.MESH
F32, BF16 = jnp.float32, jnp.bfloat16

NZ, NX, NY, NTM = 8, 4, 4, 8
CUT = 5


def tables():
    select = np.zeros((256, 576), np.float32)
    for f in range(4):
        for r in range(4):
            for s in range(16):
                for b in range(3):
                    for e in range(3):
                        rr, ss = r + b - 1, s + e - 1
                        if 0 <= rr < 4 and 0 <= ss < 16:
                            select[f * 64 + r * 16 + s, (b * 3 + e) * 64 + f * 16 + rr // 2 * 8 + ss // 2] = 1
    order_one = np.zeros((256, 256), np.float32)
    order_two = np.zeros((512, 384), np.float32)
    for core in range(2):
        for x_lo in range(2):
            for z in range(8):
                d = (core * 2 + x_lo) * 8 + z
                dp = z * 4 + x_lo * 2 + core
                for k in range(8):
                    order_one[d * 8 + k, dp * 8 + k] = 1
                for a in range(3):
                    for k in range(4):
                        order_two[d * 16 + a * 4 + k, a * 128 + dp * 4 + k] = 1
    return [jnp.asarray(m, BF16) for m in (select, select.T, order_one, order_two)]


def dot(a, b):
    return jnp.dot(a, b, preferred_element_type=F32)


def dot_nt(a, b):
    return lax.dot_general(a, b, (((1,), (1,)), ((), ())), preferred_element_type=F32)


def kernel(
    f_hbm, u_hbm, w1_hbm, w2_hbm, up_hbm, pool_hbm, ord1_hbm, ord2_hbm,
    fg_ref, g1_ref, g2_ref,
    u_ref, w1_ref, w2_ref, up_ref, pool_ref, ord1_ref, ord2_ref, s_in,
    fh, uh, um, uhm, fm, fz, ystk, ycor, u9, u9m, hid, pre_ref, back_ref, slope, p9, p9m, turned, away, away_in, part, part_in,
    sum_a, sum_b, in_a, in_b, mid_a, mid_b, mid_in_a, mid_in_b, last, last_in, own, gath,
    final, c_sum, c_in, c_mid, c_mid_in, c_end, c_end_in, d_sum, d_in, d_mid, d_mid_in, d_end, d_end_in,
    s_near, r_near, s_mate, r_mate, s_one, r_one, s_two, r_two, s_three, r_three, s_four, r_four,
    s_c1, r_c1, s_c2, r_c2, s_c3, r_c3, s_d1, r_d1, s_d2, r_d2, s_d3, r_d3,
):
    tm, dp = lax.axis_index("tm"), lax.axis_index("dp")
    y, x_hi = tm // 2, tm % 2
    z, x_lo, core = dp // 4, (dp // 2) % 2, dp % 2
    x = x_lo * 2 + x_hi

    def at(xx=x, yy=y, zz=z, cc=core):
        return {"tm": yy * 2 + xx % 2, "dp": zz * 4 + (xx // 2) * 2 + cc}

    def at_tm(t):
        return {"tm": t, "dp": dp}

    barrier = pltpu.get_barrier_semaphore()
    peers = [at_tm((tm + k) % NTM) for k in range(1, NTM)]
    peers += [at(zz=(z + k) % NZ) for k in range(1, NZ)]
    peers += [at(cc=1 - core)]
    other = (1 - x_lo) * 2
    peers += [at(xx=other), at(xx=other + 1)]
    for peer in peers:
        pl.semaphore_signal(barrier, inc=1, device_id=peer, device_id_type=MESH)

    loads = []
    order = (
        (u_hbm, u_ref), (f_hbm, fh.at[pl.ds(32, 64)]), (up_hbm, up_ref),
        (ord2_hbm, ord2_ref), (pool_hbm, pool_ref), (ord1_hbm, ord1_ref),
    )
    for i, (src, dst) in enumerate(order):
        loads.append(pltpu.make_async_copy(src, dst, s_in.at[i]))
    one, two = [], []
    for be in range(9):
        tap = pl.ds(be * 128, 128)
        one.append(pltpu.make_async_copy(w1_hbm.at[:, be], w1_ref.at[:, :, tap], s_in.at[6 + be]))
        two.append(pltpu.make_async_copy(w2_hbm.at[:, be], w2_ref.at[:, :, tap], s_in.at[15 + be]))
    for copy in loads[:2] + one + loads[2:3] + two + loads[3:]:
        copy.start()

    sent = []

    def send(src, dst, ssem, rsem, to):
        copy = pltpu.make_async_remote_copy(
            src_ref=src, dst_ref=dst, send_sem=ssem, recv_sem=rsem, device_id=to, device_id_type=MESH
        )
        copy.start()
        sent.append(copy)
        return copy

    def shifted(block, frames, ref, first):
        n = frames * 64
        column = lax.broadcasted_iota(jnp.int32, (n, 128), 0) % 16
        wide = block.astype(F32)
        back_one = jnp.where(column == 15, 0.0, pltpu.roll(wide, n - 1, 0)).astype(BF16)
        on_one = jnp.where(column == 0, 0.0, pltpu.roll(wide, 1, 0)).astype(BF16)
        zero = jnp.zeros((frames, 16, 128), BF16)
        for e, v in enumerate((back_one, block, on_one)):
            v = v.reshape(frames, 64, 128)
            for b in range(3):
                tap = slice((b * 3 + e) * 128, (b * 3 + e + 1) * 128)
                if b == 0:
                    rows = jnp.concatenate([v[:, 16:], zero], axis=1)
                elif b == 1:
                    rows = v
                else:
                    rows = jnp.concatenate([zero, v[:, :48]], axis=1)
                ref[first : first + n, tap] = rows.reshape(n, 128)

    def gate(pre, rows):
        sigma = 1.0 / (1.0 + jnp.exp(-pre))
        hid[128 + rows.start : 128 + rows.stop, :] = (pre * sigma).astype(BF16)
        slope[rows, :] = sigma * (1.0 + pre * (1.0 - sigma))

    def halves(value):
        high = value.astype(BF16)
        return high, (value - high.astype(F32)).astype(BF16)

    def keep_halves(value, ref):
        high, low = halves(value)
        n = value.shape[0]
        for be in range(9):
            tap, rows = slice(be * 128, be * 128 + 128), slice(be * 64, be * 64 + n)
            ref[rows, 0:128] = high[:, tap]
            ref[rows, 128:256] = low[:, tap]

    def widened(rows, ref):
        both = dot(up_ref[0:rows, :], ref[...])
        return both[:, 0:128] + both[:, 128:256]

    loads[0].wait()
    loads[1].wait()

    pl.semaphore_wait(barrier, len(peers))
    nxt, prv, mate = at_tm((tm + 1) % NTM), at_tm((tm + NTM - 1) % NTM), at(cc=1 - core)
    near = [
        send(fh.at[pl.ds(64, 32)], fh.at[pl.ds(0, 32)], s_near.at[0], r_near.at[0], nxt),
        send(u_ref.at[pl.ds(0, 128)], uh, s_near.at[1], r_near.at[1], prv),
    ]
    from_mate = [
        send(u_ref, um, s_mate.at[0], r_mate.at[0], mate),
        send(fh.at[pl.ds(32, 64)], fm.at[pl.ds(32, 64)], s_mate.at[1], r_mate.at[1], mate),
    ]

    ycor[...] = jnp.zeros(ycor.shape, BF16)
    hid[0:128, :] = jnp.zeros((128, 128), BF16)
    hid[384:512, :] = jnp.zeros((128, 128), BF16)
    u9[256:384, :] = jnp.zeros((128, 1152), BF16)
    p9[0:32, :] = jnp.zeros((32, 1152), BF16)
    p9[96:128, :] = jnp.zeros((32, 1152), BF16)
    shifted(u_ref[...], 4, u9, 0)
    for copy in one + loads[2:3]:
        copy.wait()
    fz[0:32, :] = jnp.zeros((32, 256), BF16)
    fz[32:96, :] = fh[32:96, :]
    cat = jnp.concatenate([fz[0:64, :], fz[16:80, :], fz[32:96, :]], axis=1)
    keep_halves(dot(cat, w1_ref[...].reshape(768, 1152)), ystk)
    pre = widened(256, ystk)
    pre_ref[...] = pre[0:128]
    gate(pre[128:256], slice(128, 256))
    for copy in two + loads[3:]:
        copy.wait()
    back = jnp.zeros((256, 128), F32)
    for a in range(3):
        back += dot_nt(u9[(2 - a) * 64 : (2 - a) * 64 + 256, :], w2_ref[a])
    back_ref[...] = back
    from_mate[0].wait_recv()
    shifted(um[...], 4, u9m, 0)

    near[0].wait_recv()

    @pl.when(tm == 0)
    def _():
        fh[0:32, :] = jnp.zeros((32, 256), BF16)

    from_mate.append(send(fh.at[pl.ds(0, 32)], fm.at[pl.ds(0, 32)], s_mate.at[2], r_mate.at[2], mate))
    head = jnp.concatenate([fh[0:16, :], fh[16:32, :]], axis=1)
    tail = jnp.concatenate([fh[16:32, :], jnp.zeros((16, 256), BF16)], axis=1)
    cat = jnp.concatenate([head, tail], axis=0)
    keep_halves(dot(cat, w1_ref[0:2].reshape(512, 1152)), ycor)
    gate(pre_ref[...] + widened(128, ycor), slice(0, 128))

    taps = jnp.concatenate([hid[a * 64 : a * 64 + 384, :] for a in range(3)], axis=1)
    away[...] = dot_nt(ord2_ref[pl.ds(pl.multiple_of((1 - core) * 256, 256), 256), :], taps).astype(BF16)
    from_mate.append(send(away, away_in, s_mate.at[3], r_mate.at[3], mate))

    near[1].wait_recv()

    @pl.when(tm == NTM - 1)
    def _():
        uh[...] = jnp.zeros((128, 128), BF16)

    from_mate.append(send(uh, uhm, s_mate.at[4], r_mate.at[4], mate))
    shifted(uh[...], 2, u9, 256)
    later = dot_nt(u9[256:384, :], w2_ref[0:2].reshape(256, 1152))
    back_ref[128:256, :] += later[:, 0:128]
    back_ref[192:256, :] += later[0:64, 128:256]
    dpre = (back_ref[...] * slope[...]).astype(BF16)
    pooled = dot(pool_ref[...], dpre).astype(BF16)
    for be in range(9):
        p9[32:96, be * 128 : be * 128 + 128] = pooled[be * 64 : be * 64 + 64]
    from_mate.append(send(p9.at[pl.ds(32, 64)], p9m, s_mate.at[5], r_mate.at[5], mate))
    turned[...] = dot_nt(ord2_ref[pl.ds(pl.multiple_of(core * 256, 256), 256), :], taps).astype(BF16)

    def put(chain, j, value):
        value = value.reshape(2, 8, 16, 128)
        for lo in range(2):
            sum_a[chain, lo * 2 + j % 2, j // 2] = value[lo, :CUT]
            sum_b[chain, j // 2, lo * 2 + j % 2] = value[lo, CUT:]

    def put_two(j, value):
        value = value.reshape(2, 8, 16, 128)
        for zz in range(NZ):
            c_sum[zz, j // 2, j % 2] = value[0, zz]
        d_sum[j // 2, j % 2] = value[1]

    def around(chain, swap):
        copies = []
        src_a, src_b, dst_a, dst_b = (mid_a, mid_b, mid_in_a, mid_in_b) if swap else (sum_a, sum_b, in_a, in_b)
        ssem, rsem = (s_two, r_two) if swap else (s_one, r_one)
        for k in range(1, 4):
            xd, yd = (x + k) % NX, (y + k) % NY
            ia, ib = (yd, xd) if swap else (xd, yd)
            to_a, to_b = (at(yy=yd), at(xx=xd)) if swap else (at(xx=xd), at(yy=yd))
            for src, dst, index, to, n in ((src_a, dst_a, ia, to_a, 2 * k - 2), (src_b, dst_b, ib, to_b, 2 * k - 1)):
                copies.append(send(src.at[chain, index], dst.at[chain, k - 1], ssem.at[chain, n], rsem.at[chain, n], to))
        return copies

    def landed(copies):
        for copy in copies:
            copy.wait_recv()

    def added(own, parts, count):
        total = own.astype(F32)
        for k in range(count):
            total += parts[k].astype(F32)
        return total.astype(BF16)

    def stage_two(chain, copies):
        landed(copies)
        mid_a[chain] = added(sum_a[chain, x], in_a.at[chain], 3)
        mid_b[chain] = added(sum_b[chain, y], in_b.at[chain], 3)
        return around(chain, True)

    def stage_three(chain, copies):
        landed(copies)
        last[chain, 0:CUT] = added(mid_a[chain, y], mid_in_a.at[chain], 3)
        last[chain, CUT:NZ] = added(mid_b[chain, x], mid_in_b.at[chain], 3)
        copies = []
        for k in range(1, NZ):
            zd = (z + k) % NZ
            copies.append(send(
                last.at[chain, zd], last_in.at[chain, k - 1], s_three.at[chain, k - 1], r_three.at[chain, k - 1], at(zz=zd)
            ))
        return copies

    def stage_four(chain, total):
        own[chain] = total
        gath[chain, tm] = total
        copies = []
        for k in range(1, NTM):
            to = at_tm((tm + k) % NTM)
            copies.append(send(own.at[chain], gath.at[chain, tm], s_four.at[chain, k - 1], r_four.at[chain, k - 1], to))
        return copies

    def within(src, dst, ssem, rsem, lo):
        def copy(slot, index, to_hi):
            return pltpu.make_async_remote_copy(
                src_ref=src.at[index], dst_ref=dst.at[slot], send_sem=ssem.at[slot], recv_sem=rsem.at[slot],
                device_id=at(xx=lo * 2 + to_hi), device_id_type=MESH,
            )

        home = (copy(0, 1 - x_hi, 1 - x_hi),)
        abroad = (copy(1, x_hi, x_hi), copy(2, 1 - x_hi, 1 - x_hi))
        return home, abroad

    def each(condition, copies, method):
        @pl.when(condition)
        def _():
            for copy in copies:
                getattr(copy, method)()

    def over_y(src, dst, ssem, rsem):
        copies = []
        for k in range(1, NY):
            yd = (y + k) % NY
            copies.append(send(src.at[yd], dst.at[k - 1], ssem.at[k - 1], rsem.at[k - 1], at(yy=yd)))
        return copies

    from_mate[1].wait_recv()
    from_mate[2].wait_recv()
    feats = []
    mine = pl.ds(pl.multiple_of(core * 128, 128), 128)
    for a in range(3):
        rows = jnp.concatenate([fh[a * 16 : a * 16 + 64, :], fm[a * 16 : a * 16 + 64, :]], axis=0)
        feats.append(dot_nt(ord1_ref[mine, :], rows).astype(BF16))
    from_mate[5].wait_recv()
    units = []
    pools = jnp.concatenate([p9[32:96, :], p9m[...]], axis=0)
    for a in range(3):
        whole = dot(feats[a], pools)
        for be in range(9):
            units.append(whole[:, be * 128 : be * 128 + 128].reshape(16, 8, 128))
            if len(units) == 2:
                tile = (a * 9 + be) // 2
                put(tile // 8, tile % 8, jnp.concatenate(units, axis=1).astype(BF16))
                units = []
                if tile == 7:
                    f1 = around(0, False)
    from_mate[4].wait_recv()
    shifted(uhm[...], 2, u9m, 256)
    from_mate[3].wait_recv()
    for first in range(0, 9, 2):
        tap = slice(first * 128, min(first * 128 + 256, 1152))
        pair = dot(turned[...], u9[:, tap]) + dot(away_in[...], u9m[:, tap])
        pair = pair.astype(BF16)
        if first == 8:
            put(1, 6, pair)
        else:
            put_two(first, pair[:, 0:128])
            put_two(first + 1, pair[:, 128:256])

    d1 = over_y(d_sum, d_in, s_d1, r_d1)
    c1 = []
    for k in range(1, NZ):
        zd = (z + k) % NZ
        c1.append(send(c_sum.at[zd], c_in.at[k - 1], s_c1.at[k - 1], r_c1.at[k - 1], at(zz=zd)))

    units.append(jnp.zeros((16, 8, 128), F32))
    put(1, 5, jnp.concatenate(units, axis=1).astype(BF16))
    put(1, 7, jnp.zeros((16, 16, 128), BF16))
    l1 = around(1, False)

    result = jnp.zeros((96, 256), F32)
    for a in range(3):
        result += dot_nt(p9[(2 - a) * 16 : (2 - a) * 16 + 96, :], w1_ref[a])
    part[...] = result
    near.append(send(part.at[pl.ds(0, 32)], part_in, s_near.at[2], r_near.at[2], prv))

    landed(d1)
    d_mid[...] = added(d_sum[y], d_in, 3)
    d_home, d_abroad = within(d_mid, d_mid_in, s_d2, r_d2, 1)
    each(x_lo == 1, d_home, "start")
    each(x_lo == 0, d_abroad, "start")
    f2 = stage_two(0, f1)
    landed(c1)
    c_mid[...] = added(c_sum[z], c_in, 7)
    c2 = over_y(c_mid, c_mid_in, s_c2, r_c2)
    l2 = stage_two(1, l1)
    f3 = stage_three(0, f2)

    d3 = []
    for k in range(1, NZ):
        zd = (z + k) % NZ
        d3.append(pltpu.make_async_remote_copy(
            src_ref=d_end.at[zd], dst_ref=d_end_in.at[k - 1], send_sem=s_d3.at[k - 1], recv_sem=r_d3.at[k - 1],
            device_id=at(zz=zd), device_id_type=MESH,
        ))

    @pl.when(x_lo == 1)
    def _():
        for copy in d_home + d_abroad:
            copy.wait_recv()
        d_end[...] = added(d_mid[x_hi], d_mid_in, 3)
        for copy in d3:
            copy.start()

    l3 = stage_three(1, l2)
    landed(c2)
    c_end[...] = added(c_mid[y], c_mid_in, 3)
    c_home, c_abroad = within(c_end, c_end_in, s_c3, r_c3, 0)
    each(x_lo == 0, c_home, "start")
    each(x_lo == 1, c_abroad, "start")
    near[2].wait_recv()
    added_late = jnp.where(tm == NTM - 1, 0.0, part_in[...])
    fg_ref[0:32, :] = part[32:64, :].astype(BF16)
    fg_ref[32:64, :] = (part[64:96, :] + added_late).astype(BF16)
    landed(f3)
    f4 = stage_four(0, added(last[0, z], last_in.at[0], 7))

    @pl.when(x_lo == 0)
    def _():
        for copy in c_home + c_abroad:
            copy.wait_recv()
        final[...] = added(c_end[x_hi], c_end_in, 3)

    @pl.when(x_lo == 1)
    def _():
        for copy in d3:
            copy.wait_recv()
        final[...] = added(d_end[z], d_end_in, 7)

    e4 = stage_four(2, final[...])
    landed(l3)
    l4 = stage_four(1, added(last[1, z], last_in.at[1], 7))

    factor = 1.0 / 256.0
    landed(e4)
    for be in range(8):
        rows = gath[2, be].astype(F32) * factor
        for a in range(3):
            g2_ref[a * 9 + be] = rows[a * 4 : a * 4 + 4]
    landed(f4)
    for tile in range(15):
        if tile == 8:
            landed(l4)
        rows = gath[tile // 8, tile % 8].astype(F32) * factor
        if tile < 14:
            g1_ref[2 * tile] = rows[0:8]
        if tile < 13:
            g1_ref[2 * tile + 1] = rows[8:16]
        if tile == 14:
            for a in range(3):
                g2_ref[a * 9 + 8] = rows[a * 4 : a * 4 + 4]
    each(x_lo == 1, d_home + tuple(d3) + c_abroad, "wait_send")
    each(x_lo == 0, d_abroad + c_home, "wait_send")
    for copy in sent:
        copy.wait_send()


def store(*refs):
    sems = refs[6]
    copies = [pltpu.make_async_copy(refs[i], refs[3 + i], sems.at[i]) for i in range(3)]
    for copy in copies:
        copy.start()
    for copy in copies:
        copy.wait()


def on_device(features, upstream, weight_one, weight_two):
    dma, vmem = pltpu.SemaphoreType.DMA, pltpu.VMEM
    tile = lambda *lead: vmem(lead + (16, 128), BF16)
    pairs = lambda shape: [dma(shape), dma(shape)]
    scratch = [
        vmem((256, 128), BF16), vmem((3, 256, 1152), BF16), vmem((3, 128, 1152), BF16),
        vmem((256, 576), BF16), vmem((576, 256), BF16), vmem((256, 256), BF16), vmem((512, 384), BF16), dma((24,)),
        vmem((96, 256), BF16), vmem((128, 128), BF16), vmem((256, 128), BF16), vmem((128, 128), BF16),
        vmem((96, 256), BF16), vmem((96, 256), BF16),
        vmem((576, 256), BF16), vmem((576, 256), BF16), vmem((384, 1152), BF16), vmem((384, 1152), BF16),
        vmem((512, 128), BF16), vmem((128, 128), F32), vmem((256, 128), F32), vmem((256, 128), F32),
        vmem((128, 1152), BF16), vmem((64, 1152), BF16),
        vmem((256, 384), BF16), vmem((256, 384), BF16), vmem((256, 384), BF16),
        vmem((96, 256), F32), vmem((32, 256), F32),
        tile(2, NX, NY, CUT), tile(2, NY, NX, NZ - CUT), tile(2, 3, NY, CUT), tile(2, 3, NX, NZ - CUT),
        tile(2, NY, CUT), tile(2, NX, NZ - CUT), tile(2, 3, CUT), tile(2, 3, NZ - CUT),
        tile(2, NZ), tile(2, NZ - 1), tile(3), tile(3, NTM),
        tile(), tile(NZ, NY, 2), tile(NZ - 1, NY, 2), tile(NY, 2), tile(3, 2), tile(2), tile(3),
        tile(NY, 2, NZ), tile(3, 2, NZ), tile(2, NZ), tile(3, NZ), tile(NZ), tile(NZ - 1),
    ]
    scratch += pairs((3,)) + pairs((6,)) + pairs((2, 6)) * 2 + pairs((2, 7)) + pairs((3, 7))
    scratch += pairs((7,)) + pairs((3,)) * 4 + pairs((7,))
    spec = pl.BlockSpec(memory_space=pltpu.VMEM)
    shapes = (
        jax.ShapeDtypeStruct((64, 256), BF16),
        jax.ShapeDtypeStruct((27, 8, 128), F32),
        jax.ShapeDtypeStruct((27, 4, 128), F32),
    )
    results = pl.pallas_call(
        kernel,
        out_shape=shapes,
        in_specs=[pl.BlockSpec(memory_space=pltpu.HBM)] * 8,
        out_specs=(spec,) * 3,
        scratch_shapes=scratch,
        compiler_params=pltpu.CompilerParams(
            collective_id=0, has_side_effects=True, vmem_limit_bytes=24 * 1024 * 1024
        ),
    )(
        *(
            pltpu.with_memory_space_constraint(v, pltpu.HBM)
            for v in (
                features.reshape(64, 256),
                upstream.reshape(256, 128),
                weight_one.reshape(3, 9, 256, 128),
                weight_two.reshape(3, 9, 128, 128),
                *tables(),
            )
        )
    )
    fg, one, two = pl.pallas_call(
        store,
        out_shape=shapes,
        in_specs=[spec] * 3,
        out_specs=(pl.BlockSpec(memory_space=pltpu.HBM),) * 3,
        scratch_shapes=[dma((3,))],
    )(*(pltpu.with_memory_space_constraint(v, pltpu.VMEM) for v in results))
    return (
        fg.reshape(features.shape),
        one.reshape(3, 3, 3, 8, 128),
        two.reshape(3, 3, 3, 4, 128),
    )


def solution(mesh):
    wide = P("dp", "tm", None, None, None)
    cut = P(None, None, None, "dp", None)
    return jax.shard_map(
        on_device, mesh=mesh, in_specs=(wide, wide, P(), P()), out_specs=(wide, cut, cut), check_vma=False
    )
```

```python
import jax
import jax.numpy as jnp
import numpy as np
from jax import lax
from jax.experimental import pallas as pl
from jax.experimental.pallas import tpu as pltpu
from jax.sharding import PartitionSpec as P

MESH = pl.DeviceIdType.MESH
F32, BF16 = jnp.float32, jnp.bfloat16

NZ, NX, NY, NTM = 8, 4, 4, 8
FAR_Z, FAR_TM = (4, 3, 5, 2, 6, 1, 7), (5, 3, 4, 1, 7, 2, 6)
CUT = 5


def tables():
    select = np.zeros((256, 576), np.float32)
    for f in range(4):
        for r in range(4):
            for s in range(16):
                for b in range(3):
                    for e in range(3):
                        rr, ss = r + b - 1, s + e - 1
                        if 0 <= rr < 4 and 0 <= ss < 16:
                            select[f * 64 + r * 16 + s, (b * 3 + e) * 64 + f * 16 + rr // 2 * 8 + ss // 2] = 1
    order_one = np.zeros((256, 256), np.float32)
    order_two = np.zeros((512, 384), np.float32)
    for core in range(2):
        for x_lo in range(2):
            for z in range(8):
                d = (core * 2 + x_lo) * 8 + z
                dp = z * 4 + x_lo * 2 + core
                for k in range(8):
                    order_one[d * 8 + k, dp * 8 + k] = 1
                for a in range(3):
                    for k in range(4):
                        order_two[d * 16 + a * 4 + k, a * 128 + dp * 4 + k] = 1
    return [jnp.asarray(m, BF16) for m in (select, select.T, order_one, order_two)]


def dot(a, b):
    return jnp.dot(a, b, preferred_element_type=F32)


def dot_nt(a, b):
    return lax.dot_general(a, b, (((1,), (1,)), ((), ())), preferred_element_type=F32)


def kernel(
    f_hbm, u_hbm, w1_hbm, w2_hbm, up_hbm, pool_hbm, ord1_hbm, ord2_hbm,
    fg_ref, g1_ref, g2_ref,
    u_ref, w1_ref, w2_ref, up_ref, pool_ref, ord1_ref, ord2_ref, s_in,
    fh, uh, um, uhm, fm, fz, ystk, ycor, u9, u9m, hid, pre_ref, back_ref, slope, p9, p9m, turned, away, away_in, part, part_in,
    sum_a, sum_b, in_a, in_b, mid_a, mid_b, mid_in_a, mid_in_b, last, last_in, own, gath,
    final, c_sum, c_in, c_mid, c_mid_in, c_end, c_end_in, d_sum, d_in, d_mid, d_mid_in, d_end, d_end_in,
    s_near, r_near, s_mate, r_mate, s_one, r_one, s_two, r_two, s_three, r_three, s_four, r_four,
    s_c1, r_c1, s_c2, r_c2, s_c3, r_c3, s_d1, r_d1, s_d2, r_d2, s_d3, r_d3,
):
    tm, dp = lax.axis_index("tm"), lax.axis_index("dp")
    y, x_hi = tm // 2, tm % 2
    z, x_lo, core = dp // 4, (dp // 2) % 2, dp % 2
    x = x_lo * 2 + x_hi

    def at(xx=x, yy=y, zz=z, cc=core):
        return {"tm": yy * 2 + xx % 2, "dp": zz * 4 + (xx // 2) * 2 + cc}

    def at_tm(t):
        return {"tm": t, "dp": dp}

    barrier = pltpu.get_barrier_semaphore()
    peers = [at_tm((tm + k) % NTM) for k in range(1, NTM)]
    peers += [at(zz=(z + k) % NZ) for k in range(1, NZ)]
    peers += [at(cc=1 - core)]
    other = (1 - x_lo) * 2
    peers += [at(xx=other), at(xx=other + 1)]
    for peer in peers:
        pl.semaphore_signal(barrier, inc=1, device_id=peer, device_id_type=MESH)

    loads = []
    order = (
        (u_hbm, u_ref), (f_hbm, fh.at[pl.ds(32, 64)]), (up_hbm, up_ref),
        (ord2_hbm, ord2_ref), (pool_hbm, pool_ref), (ord1_hbm, ord1_ref),
    )
    for i, (src, dst) in enumerate(order):
        loads.append(pltpu.make_async_copy(src, dst, s_in.at[i]))
    one, two = [], []
    for be in range(9):
        tap = pl.ds(be * 128, 128)
        one.append(pltpu.make_async_copy(w1_hbm.at[:, be], w1_ref.at[:, :, tap], s_in.at[6 + be]))
        two.append(pltpu.make_async_copy(w2_hbm.at[:, be], w2_ref.at[:, :, tap], s_in.at[15 + be]))
    for copy in loads[:2] + one + loads[2:3] + two + loads[3:]:
        copy.start()

    sent = []

    def send(src, dst, ssem, rsem, to):
        copy = pltpu.make_async_remote_copy(
            src_ref=src, dst_ref=dst, send_sem=ssem, recv_sem=rsem, device_id=to, device_id_type=MESH
        )
        copy.start()
        sent.append(copy)
        return copy

    def shifted(block, frames, ref, first):
        n = frames * 64
        column = lax.broadcasted_iota(jnp.int32, (n, 128), 0) % 16
        wide = block.astype(F32)
        back_one = jnp.where(column == 15, 0.0, pltpu.roll(wide, n - 1, 0)).astype(BF16)
        on_one = jnp.where(column == 0, 0.0, pltpu.roll(wide, 1, 0)).astype(BF16)
        zero = jnp.zeros((frames, 16, 128), BF16)
        for e, v in enumerate((back_one, block, on_one)):
            v = v.reshape(frames, 64, 128)
            for b in range(3):
                tap = slice((b * 3 + e) * 128, (b * 3 + e + 1) * 128)
                if b == 0:
                    rows = jnp.concatenate([v[:, 16:], zero], axis=1)
                elif b == 1:
                    rows = v
                else:
                    rows = jnp.concatenate([zero, v[:, :48]], axis=1)
                ref[first : first + n, tap] = rows.reshape(n, 128)

    def gate(pre, rows):
        sigma = 1.0 / (1.0 + jnp.exp(-pre))
        hid[128 + rows.start : 128 + rows.stop, :] = (pre * sigma).astype(BF16)
        slope[rows, :] = sigma * (1.0 + pre * (1.0 - sigma))

    def halves(value):
        high = value.astype(BF16)
        return high, (value - high.astype(F32)).astype(BF16)

    def keep_halves(value, ref):
        high, low = halves(value)
        n = value.shape[0]
        for be in range(9):
            tap, rows = slice(be * 128, be * 128 + 128), slice(be * 64, be * 64 + n)
            ref[rows, 0:128] = high[:, tap]
            ref[rows, 128:256] = low[:, tap]

    def widened(rows, ref):
        both = dot(up_ref[0:rows, :], ref[...])
        return both[:, 0:128] + both[:, 128:256]

    loads[0].wait()
    loads[1].wait()

    pl.semaphore_wait(barrier, len(peers))
    nxt, prv, mate = at_tm((tm + 1) % NTM), at_tm((tm + NTM - 1) % NTM), at(cc=1 - core)
    near = [
        send(fh.at[pl.ds(64, 32)], fh.at[pl.ds(0, 32)], s_near.at[0], r_near.at[0], nxt),
        send(u_ref.at[pl.ds(0, 128)], uh, s_near.at[1], r_near.at[1], prv),
    ]
    from_mate = [
        send(u_ref, um, s_mate.at[0], r_mate.at[0], mate),
        send(fh.at[pl.ds(32, 64)], fm.at[pl.ds(32, 64)], s_mate.at[1], r_mate.at[1], mate),
    ]

    ycor[...] = jnp.zeros(ycor.shape, BF16)
    hid[0:128, :] = jnp.zeros((128, 128), BF16)
    hid[384:512, :] = jnp.zeros((128, 128), BF16)
    u9[256:384, :] = jnp.zeros((128, 1152), BF16)
    p9[0:32, :] = jnp.zeros((32, 1152), BF16)
    p9[96:128, :] = jnp.zeros((32, 1152), BF16)
    shifted(u_ref[...], 4, u9, 0)
    for copy in one + loads[2:3]:
        copy.wait()
    fz[0:32, :] = jnp.zeros((32, 256), BF16)
    fz[32:96, :] = fh[32:96, :]
    cat = jnp.concatenate([fz[0:64, :], fz[16:80, :], fz[32:96, :]], axis=1)
    keep_halves(dot(cat, w1_ref[...].reshape(768, 1152)), ystk)
    pre = widened(256, ystk)
    pre_ref[...] = pre[0:128]
    gate(pre[128:256], slice(128, 256))
    for copy in two + loads[3:]:
        copy.wait()
    back = jnp.zeros((256, 128), F32)
    for a in range(3):
        back += dot_nt(u9[(2 - a) * 64 : (2 - a) * 64 + 256, :], w2_ref[a])
    back_ref[...] = back
    from_mate[0].wait_recv()
    shifted(um[...], 4, u9m, 0)

    near[0].wait_recv()

    @pl.when(tm == 0)
    def _():
        fh[0:32, :] = jnp.zeros((32, 256), BF16)

    from_mate.append(send(fh.at[pl.ds(0, 32)], fm.at[pl.ds(0, 32)], s_mate.at[2], r_mate.at[2], mate))
    head = jnp.concatenate([fh[0:16, :], fh[16:32, :]], axis=1)
    tail = jnp.concatenate([fh[16:32, :], jnp.zeros((16, 256), BF16)], axis=1)
    cat = jnp.concatenate([head, tail], axis=0)
    keep_halves(dot(cat, w1_ref[0:2].reshape(512, 1152)), ycor)
    gate(pre_ref[...] + widened(128, ycor), slice(0, 128))

    taps = jnp.concatenate([hid[a * 64 : a * 64 + 384, :] for a in range(3)], axis=1)
    away[...] = dot_nt(ord2_ref[pl.ds(pl.multiple_of((1 - core) * 256, 256), 256), :], taps).astype(BF16)
    from_mate.append(send(away, away_in, s_mate.at[3], r_mate.at[3], mate))

    near[1].wait_recv()

    @pl.when(tm == NTM - 1)
    def _():
        uh[...] = jnp.zeros((128, 128), BF16)

    from_mate.append(send(uh, uhm, s_mate.at[4], r_mate.at[4], mate))
    shifted(uh[...], 2, u9, 256)
    later = dot_nt(u9[256:384, :], w2_ref[0:2].reshape(256, 1152))
    back_ref[128:256, :] += later[:, 0:128]
    back_ref[192:256, :] += later[0:64, 128:256]
    dpre = (back_ref[...] * slope[...]).astype(BF16)
    pooled = dot(pool_ref[...], dpre).astype(BF16)
    for be in range(9):
        p9[32:96, be * 128 : be * 128 + 128] = pooled[be * 64 : be * 64 + 64]
    from_mate.append(send(p9.at[pl.ds(32, 64)], p9m, s_mate.at[5], r_mate.at[5], mate))
    turned[...] = dot_nt(ord2_ref[pl.ds(pl.multiple_of(core * 256, 256), 256), :], taps).astype(BF16)

    def put(chain, j, value):
        value = value.reshape(2, 8, 16, 128)
        for lo in range(2):
            sum_a[chain, lo * 2 + j % 2, j // 2] = value[lo, :CUT]
            sum_b[chain, j // 2, lo * 2 + j % 2] = value[lo, CUT:]

    def put_two(j, value):
        value = value.reshape(2, 8, 16, 128)
        for zz in range(NZ):
            c_sum[zz, j // 2, j % 2] = value[0, zz]
        d_sum[j // 2, j % 2] = value[1]

    def around(chain, swap):
        copies = []
        src_a, src_b, dst_a, dst_b = (mid_a, mid_b, mid_in_a, mid_in_b) if swap else (sum_a, sum_b, in_a, in_b)
        ssem, rsem = (s_two, r_two) if swap else (s_one, r_one)
        for k in (1, 2, 3, 0) if swap else (1, 2, 3):
            xd, yd = (x + k) % NX, (y + k) % NY
            ia, ib = (yd, xd) if swap else (xd, yd)
            to_a, to_b = (at(yy=yd), at(xx=xd)) if swap else (at(xx=xd), at(yy=yd))
            for src, dst, index, to, n in ((src_a, dst_a, ia, to_a, 2 * k - 2), (src_b, dst_b, ib, to_b, 2 * k - 1)):
                if swap:
                    held, parts, place = (sum_a, in_a, x) if src is src_a else (sum_b, in_b, y)
                    total = held[chain, place, index].astype(F32)
                    for m in range(3):
                        total += parts[chain, m, index].astype(F32)
                    src[chain, index] = total.astype(BF16)
                if k:
                    copies.append(
                        send(src.at[chain, index], dst.at[chain, k - 1], ssem.at[chain, n], rsem.at[chain, n], to)
                    )
        return copies

    def landed(copies):
        for copy in copies:
            copy.wait_recv()

    def added(own, parts, count):
        total = own.astype(F32)
        for k in range(count):
            total += parts[k].astype(F32)
        return total.astype(BF16)

    def stage_two(chain, copies):
        landed(copies)
        return around(chain, True)

    def stage_three(chain, copies):
        landed(copies)
        last[chain, 0:CUT] = added(mid_a[chain, y], mid_in_a.at[chain], 3)
        last[chain, CUT:NZ] = added(mid_b[chain, x], mid_in_b.at[chain], 3)
        copies = []
        for k in FAR_Z:
            zd = (z + k) % NZ
            copies.append(send(
                last.at[chain, zd], last_in.at[chain, k - 1], s_three.at[chain, k - 1], r_three.at[chain, k - 1], at(zz=zd)
            ))
        return copies

    def stage_four(chain, total):
        own[chain] = total
        gath[chain, tm] = total
        copies = []
        for k in FAR_TM:
            to = at_tm((tm + k) % NTM)
            copies.append(send(own.at[chain], gath.at[chain, tm], s_four.at[chain, k - 1], r_four.at[chain, k - 1], to))
        return copies

    def within(src, dst, ssem, rsem, lo):
        def copy(slot, index, to_hi):
            return pltpu.make_async_remote_copy(
                src_ref=src.at[index], dst_ref=dst.at[slot], send_sem=ssem.at[slot], recv_sem=rsem.at[slot],
                device_id=at(xx=lo * 2 + to_hi), device_id_type=MESH,
            )

        home = (copy(0, 1 - x_hi, 1 - x_hi),)
        abroad = (copy(1, x_hi, x_hi), copy(2, 1 - x_hi, 1 - x_hi))
        return home, abroad

    def each(condition, copies, method):
        @pl.when(condition)
        def _():
            for copy in copies:
                getattr(copy, method)()

    def over_y(src, dst, ssem, rsem):
        copies = []
        for k in range(1, NY):
            yd = (y + k) % NY
            copies.append(send(src.at[yd], dst.at[k - 1], ssem.at[k - 1], rsem.at[k - 1], at(yy=yd)))
        return copies

    from_mate[1].wait_recv()
    from_mate[2].wait_recv()
    feats = []
    mine = pl.ds(pl.multiple_of(core * 128, 128), 128)
    for a in range(3):
        rows = jnp.concatenate([fh[a * 16 : a * 16 + 64, :], fm[a * 16 : a * 16 + 64, :]], axis=0)
        feats.append(dot_nt(ord1_ref[mine, :], rows).astype(BF16))
    from_mate[5].wait_recv()
    units = []
    pools = jnp.concatenate([p9[32:96, :], p9m[...]], axis=0)
    for a in range(3):
        whole = dot(feats[a], pools)
        for be in range(9):
            units.append(whole[:, be * 128 : be * 128 + 128].reshape(16, 8, 128))
            if len(units) == 2:
                tile = (a * 9 + be) // 2
                put(tile // 8, tile % 8, jnp.concatenate(units, axis=1).astype(BF16))
                units = []
                if tile == 7:
                    f1 = around(0, False)
    from_mate[4].wait_recv()
    shifted(uhm[...], 2, u9m, 256)
    from_mate[3].wait_recv()
    for first in range(0, 9, 2):
        tap = slice(first * 128, min(first * 128 + 256, 1152))
        pair = dot(turned[...], u9[:, tap]) + dot(away_in[...], u9m[:, tap])
        pair = pair.astype(BF16)
        if first == 8:
            put(1, 6, pair)
        else:
            put_two(first, pair[:, 0:128])
            put_two(first + 1, pair[:, 128:256])

    d1 = over_y(d_sum, d_in, s_d1, r_d1)
    c1 = []
    for k in FAR_Z:
        zd = (z + k) % NZ
        c1.append(send(c_sum.at[zd], c_in.at[k - 1], s_c1.at[k - 1], r_c1.at[k - 1], at(zz=zd)))

    units.append(jnp.zeros((16, 8, 128), F32))
    put(1, 5, jnp.concatenate(units, axis=1).astype(BF16))
    put(1, 7, jnp.zeros((16, 16, 128), BF16))
    l1 = around(1, False)

    result = jnp.zeros((96, 256), F32)
    for a in range(3):
        result += dot_nt(p9[(2 - a) * 16 : (2 - a) * 16 + 96, :], w1_ref[a])
    part[...] = result
    near.append(send(part.at[pl.ds(0, 32)], part_in, s_near.at[2], r_near.at[2], prv))

    landed(d1)
    d_mid[...] = added(d_sum[y], d_in, 3)
    d_home, d_abroad = within(d_mid, d_mid_in, s_d2, r_d2, 1)
    each(x_lo == 1, d_home, "start")
    each(x_lo == 0, d_abroad, "start")
    f2 = stage_two(0, f1)
    l2 = stage_two(1, l1)
    landed(c1)
    c_mid[...] = added(c_sum[z], c_in, 7)
    c2 = over_y(c_mid, c_mid_in, s_c2, r_c2)
    f3 = stage_three(0, f2)

    d3 = []
    for k in FAR_Z:
        zd = (z + k) % NZ
        d3.append(pltpu.make_async_remote_copy(
            src_ref=d_end.at[zd], dst_ref=d_end_in.at[k - 1], send_sem=s_d3.at[k - 1], recv_sem=r_d3.at[k - 1],
            device_id=at(zz=zd), device_id_type=MESH,
        ))

    @pl.when(x_lo == 1)
    def _():
        for copy in d_home + d_abroad:
            copy.wait_recv()
        d_end[...] = added(d_mid[x_hi], d_mid_in, 3)
        for copy in d3:
            copy.start()

    l3 = stage_three(1, l2)
    landed(c2)
    c_end[...] = added(c_mid[y], c_mid_in, 3)
    c_home, c_abroad = within(c_end, c_end_in, s_c3, r_c3, 0)
    each(x_lo == 0, c_home, "start")
    each(x_lo == 1, c_abroad, "start")
    near[2].wait_recv()
    added_late = jnp.where(tm == NTM - 1, 0.0, part_in[...])
    fg_ref[0:32, :] = part[32:64, :].astype(BF16)
    fg_ref[32:64, :] = (part[64:96, :] + added_late).astype(BF16)
    landed(f3)
    f4 = stage_four(0, added(last[0, z], last_in.at[0], 7))

    @pl.when(x_lo == 0)
    def _():
        for copy in c_home + c_abroad:
            copy.wait_recv()
        final[...] = added(c_end[x_hi], c_end_in, 3)

    @pl.when(x_lo == 1)
    def _():
        for copy in d3:
            copy.wait_recv()
        final[...] = added(d_end[z], d_end_in, 7)

    e4 = stage_four(2, final[...])
    landed(l3)
    l4 = stage_four(1, added(last[1, z], last_in.at[1], 7))

    factor = 1.0 / 256.0
    landed(e4)
    for be in range(8):
        rows = gath[2, be].astype(F32) * factor
        for a in range(3):
            g2_ref[a * 9 + be] = rows[a * 4 : a * 4 + 4]
    landed(f4)
    for tile in range(15):
        if tile == 8:
            landed(l4)
        rows = gath[tile // 8, tile % 8].astype(F32) * factor
        if tile < 14:
            g1_ref[2 * tile] = rows[0:8]
        if tile < 13:
            g1_ref[2 * tile + 1] = rows[8:16]
        if tile == 14:
            for a in range(3):
                g2_ref[a * 9 + 8] = rows[a * 4 : a * 4 + 4]
    each(x_lo == 1, d_home + tuple(d3) + c_abroad, "wait_send")
    each(x_lo == 0, d_abroad + c_home, "wait_send")
    for copy in sent:
        copy.wait_send()


def store(*refs):
    sems = refs[6]
    copies = [pltpu.make_async_copy(refs[i], refs[3 + i], sems.at[i]) for i in range(3)]
    for copy in copies:
        copy.start()
    for copy in copies:
        copy.wait()


def on_device(features, upstream, weight_one, weight_two):
    dma, vmem = pltpu.SemaphoreType.DMA, pltpu.VMEM
    tile = lambda *lead: vmem(lead + (16, 128), BF16)
    pairs = lambda shape: [dma(shape), dma(shape)]
    scratch = [
        vmem((256, 128), BF16), vmem((3, 256, 1152), BF16), vmem((3, 128, 1152), BF16),
        vmem((256, 576), BF16), vmem((576, 256), BF16), vmem((256, 256), BF16), vmem((512, 384), BF16), dma((24,)),
        vmem((96, 256), BF16), vmem((128, 128), BF16), vmem((256, 128), BF16), vmem((128, 128), BF16),
        vmem((96, 256), BF16), vmem((96, 256), BF16),
        vmem((576, 256), BF16), vmem((576, 256), BF16), vmem((384, 1152), BF16), vmem((384, 1152), BF16),
        vmem((512, 128), BF16), vmem((128, 128), F32), vmem((256, 128), F32), vmem((256, 128), F32),
        vmem((128, 1152), BF16), vmem((64, 1152), BF16),
        vmem((256, 384), BF16), vmem((256, 384), BF16), vmem((256, 384), BF16),
        vmem((96, 256), F32), vmem((32, 256), F32),
        tile(2, NX, NY, CUT), tile(2, NY, NX, NZ - CUT), tile(2, 3, NY, CUT), tile(2, 3, NX, NZ - CUT),
        tile(2, NY, CUT), tile(2, NX, NZ - CUT), tile(2, 3, CUT), tile(2, 3, NZ - CUT),
        tile(2, NZ), tile(2, NZ - 1), tile(3), tile(3, NTM),
        tile(), tile(NZ, NY, 2), tile(NZ - 1, NY, 2), tile(NY, 2), tile(3, 2), tile(2), tile(3),
        tile(NY, 2, NZ), tile(3, 2, NZ), tile(2, NZ), tile(3, NZ), tile(NZ), tile(NZ - 1),
    ]
    scratch += pairs((3,)) + pairs((6,)) + pairs((2, 6)) * 2 + pairs((2, 7)) + pairs((3, 7))
    scratch += pairs((7,)) + pairs((3,)) * 4 + pairs((7,))
    spec = pl.BlockSpec(memory_space=pltpu.VMEM)
    shapes = (
        jax.ShapeDtypeStruct((64, 256), BF16),
        jax.ShapeDtypeStruct((27, 8, 128), F32),
        jax.ShapeDtypeStruct((27, 4, 128), F32),
    )
    results = pl.pallas_call(
        kernel,
        out_shape=shapes,
        in_specs=[pl.BlockSpec(memory_space=pltpu.HBM)] * 8,
        out_specs=(spec,) * 3,
        scratch_shapes=scratch,
        compiler_params=pltpu.CompilerParams(
            collective_id=0, has_side_effects=True, vmem_limit_bytes=24 * 1024 * 1024
        ),
    )(
        *(
            pltpu.with_memory_space_constraint(v, pltpu.HBM)
            for v in (
                features.reshape(64, 256),
                upstream.reshape(256, 128),
                weight_one.reshape(3, 9, 256, 128),
                weight_two.reshape(3, 9, 128, 128),
                *tables(),
            )
        )
    )
    fg, one, two = pl.pallas_call(
        store,
        out_shape=shapes,
        in_specs=[spec] * 3,
        out_specs=(pl.BlockSpec(memory_space=pltpu.HBM),) * 3,
        scratch_shapes=[dma((3,))],
    )(*(pltpu.with_memory_space_constraint(v, pltpu.VMEM) for v in results))
    return (
        fg.reshape(features.shape),
        one.reshape(3, 3, 3, 8, 128),
        two.reshape(3, 3, 3, 4, 128),
    )


def solution(mesh):
    wide = P("dp", "tm", None, None, None)
    cut = P(None, None, None, "dp", None)
    return jax.shard_map(
        on_device, mesh=mesh, in_specs=(wide, wide, P(), P()), out_specs=(wide, cut, cut), check_vma=False
    )
```

```python
import jax
import jax.numpy as jnp
import numpy as np
from jax import lax
from jax.experimental import pallas as pl
from jax.experimental.pallas import tpu as pltpu
from jax.sharding import PartitionSpec as P

MESH = pl.DeviceIdType.MESH
F32, BF16 = jnp.float32, jnp.bfloat16

NZ, NX, NY, NTM = 8, 4, 4, 8
FAR_Z, FAR_TM = (4, 3, 5, 2, 6, 1, 7), (5, 3, 4, 1, 7, 2, 6)
CUT = 5


def tables():
    select = np.zeros((256, 576), np.float32)
    for f in range(4):
        for r in range(4):
            for s in range(16):
                for b in range(3):
                    for e in range(3):
                        rr, ss = r + b - 1, s + e - 1
                        if 0 <= rr < 4 and 0 <= ss < 16:
                            select[f * 64 + r * 16 + s, (b * 3 + e) * 64 + f * 16 + rr // 2 * 8 + ss // 2] = 1
    order_one = np.zeros((256, 256), np.float32)
    order_two = np.zeros((512, 384), np.float32)
    for core in range(2):
        for x_lo in range(2):
            for z in range(8):
                d = (core * 2 + x_lo) * 8 + z
                dp = z * 4 + x_lo * 2 + core
                for k in range(8):
                    order_one[d * 8 + k, dp * 8 + k] = 1
                for a in range(3):
                    for k in range(4):
                        order_two[d * 16 + a * 4 + k, a * 128 + dp * 4 + k] = 1
    return [jnp.asarray(m, BF16) for m in (select, select.T, order_one, order_two)]


def dot(a, b):
    return jnp.dot(a, b, preferred_element_type=F32)


def dot_nt(a, b):
    return lax.dot_general(a, b, (((1,), (1,)), ((), ())), preferred_element_type=F32)


def kernel(
    f_hbm, u_hbm, w1_hbm, w2_hbm, up_hbm, pool_hbm, ord1_hbm, ord2_hbm,
    fg_ref, g1_ref, g2_ref,
    u_ref, w1_ref, w2_ref, up_ref, pool_ref, ord1_ref, ord2_ref, s_in,
    fh, uh, um, uhm, fm, fz, ystk, ycor, u9, u9m, hid, pre_ref, back_ref, slope, p9, p9m, turned, away, away_in, part, part_in,
    sum_a, sum_b, in_a, in_b, mid_a, mid_b, mid_in_a, mid_in_b, last, last_in, own, gath,
    final, c_sum, c_in, c_mid, c_mid_in, c_end, c_end_in, d_sum, d_in, d_mid, d_mid_in, d_end, d_end_in,
    s_near, r_near, s_mate, r_mate, s_one, r_one, s_two, r_two, s_three, r_three, s_four, r_four,
    s_c1, r_c1, s_c2, r_c2, s_c3, r_c3, s_d1, r_d1, s_d2, r_d2, s_d3, r_d3,
):
    tm, dp = lax.axis_index("tm"), lax.axis_index("dp")
    y, x_hi = tm // 2, tm % 2
    z, x_lo, core = dp // 4, (dp // 2) % 2, dp % 2
    x = x_lo * 2 + x_hi

    def at(xx=x, yy=y, zz=z, cc=core):
        return {"tm": yy * 2 + xx % 2, "dp": zz * 4 + (xx // 2) * 2 + cc}

    def at_tm(t):
        return {"tm": t, "dp": dp}

    barrier = pltpu.get_barrier_semaphore()
    peers = [at_tm((tm + k) % NTM) for k in range(1, NTM)]
    peers += [at(zz=(z + k) % NZ) for k in range(1, NZ)]
    peers += [at(cc=1 - core)]
    other = (1 - x_lo) * 2
    peers += [at(xx=other), at(xx=other + 1)]
    for peer in peers:
        pl.semaphore_signal(barrier, inc=1, device_id=peer, device_id_type=MESH)

    loads = []
    order = (
        (u_hbm, u_ref), (f_hbm, fh.at[pl.ds(32, 64)]), (up_hbm, up_ref),
        (ord2_hbm, ord2_ref), (pool_hbm, pool_ref), (ord1_hbm, ord1_ref),
    )
    for i, (src, dst) in enumerate(order):
        loads.append(pltpu.make_async_copy(src, dst, s_in.at[i]))
    one, two = [], []
    for be in range(9):
        tap = pl.ds(be * 128, 128)
        one.append(pltpu.make_async_copy(w1_hbm.at[:, be], w1_ref.at[:, :, tap], s_in.at[6 + be]))
        two.append(pltpu.make_async_copy(w2_hbm.at[:, be], w2_ref.at[:, :, tap], s_in.at[15 + be]))
    for copy in loads[:2] + one + loads[2:3] + two + loads[3:]:
        copy.start()

    sent = []

    def send(src, dst, ssem, rsem, to):
        copy = pltpu.make_async_remote_copy(
            src_ref=src, dst_ref=dst, send_sem=ssem, recv_sem=rsem, device_id=to, device_id_type=MESH
        )
        copy.start()
        sent.append(copy)
        return copy

    def shifted(block, frames, ref, first):
        n = frames * 64
        column = lax.broadcasted_iota(jnp.int32, (n, 128), 0) % 16
        wide = block.astype(F32)
        back_one = jnp.where(column == 15, 0.0, pltpu.roll(wide, n - 1, 0)).astype(BF16)
        on_one = jnp.where(column == 0, 0.0, pltpu.roll(wide, 1, 0)).astype(BF16)
        zero = jnp.zeros((frames, 16, 128), BF16)
        for e, v in enumerate((back_one, block, on_one)):
            v = v.reshape(frames, 64, 128)
            for b in range(3):
                tap = slice((b * 3 + e) * 128, (b * 3 + e + 1) * 128)
                if b == 0:
                    rows = jnp.concatenate([v[:, 16:], zero], axis=1)
                elif b == 1:
                    rows = v
                else:
                    rows = jnp.concatenate([zero, v[:, :48]], axis=1)
                ref[first : first + n, tap] = rows.reshape(n, 128)

    def gate(pre, rows):
        sigma = 1.0 / (1.0 + jnp.exp(-pre))
        hid[128 + rows.start : 128 + rows.stop, :] = (pre * sigma).astype(BF16)
        slope[rows, :] = sigma * (1.0 + pre * (1.0 - sigma))

    def halves(value):
        high = value.astype(BF16)
        return high, (value - high.astype(F32)).astype(BF16)

    def keep_halves(value, ref):
        high, low = halves(value)
        n = value.shape[0]
        for be in range(9):
            tap, rows = slice(be * 128, be * 128 + 128), slice(be * 64, be * 64 + n)
            ref[rows, 0:128] = high[:, tap]
            ref[rows, 128:256] = low[:, tap]

    def widened(rows, ref):
        both = dot(up_ref[0:rows, :], ref[...])
        return both[:, 0:128] + both[:, 128:256]

    loads[0].wait()
    loads[1].wait()

    pl.semaphore_wait(barrier, len(peers))
    nxt, prv, mate = at_tm((tm + 1) % NTM), at_tm((tm + NTM - 1) % NTM), at(cc=1 - core)
    near = [
        send(fh.at[pl.ds(64, 32)], fh.at[pl.ds(0, 32)], s_near.at[0], r_near.at[0], nxt),
        send(u_ref.at[pl.ds(0, 128)], uh, s_near.at[1], r_near.at[1], prv),
    ]
    from_mate = [
        send(u_ref, um, s_mate.at[0], r_mate.at[0], mate),
        send(fh.at[pl.ds(32, 64)], fm.at[pl.ds(32, 64)], s_mate.at[1], r_mate.at[1], mate),
    ]

    ycor[...] = jnp.zeros(ycor.shape, BF16)
    hid[0:128, :] = jnp.zeros((128, 128), BF16)
    hid[384:512, :] = jnp.zeros((128, 128), BF16)
    u9[256:384, :] = jnp.zeros((128, 1152), BF16)
    p9[0:32, :] = jnp.zeros((32, 1152), BF16)
    p9[96:128, :] = jnp.zeros((32, 1152), BF16)
    shifted(u_ref[...], 4, u9, 0)
    for copy in one + loads[2:3]:
        copy.wait()
    fz[0:32, :] = jnp.zeros((32, 256), BF16)
    fz[32:96, :] = fh[32:96, :]
    cat = jnp.concatenate([fz[0:64, :], fz[16:80, :], fz[32:96, :]], axis=1)
    keep_halves(dot(cat, w1_ref[...].reshape(768, 1152)), ystk)
    pre = widened(256, ystk)
    pre_ref[...] = pre[0:128]
    gate(pre[128:256], slice(128, 256))
    for copy in two + loads[3:]:
        copy.wait()
    back = jnp.zeros((256, 128), F32)
    for a in range(3):
        back += dot_nt(u9[(2 - a) * 64 : (2 - a) * 64 + 256, :], w2_ref[a])
    back_ref[...] = back
    from_mate[0].wait_recv()
    shifted(um[...], 4, u9m, 0)

    near[0].wait_recv()

    @pl.when(tm == 0)
    def _():
        fh[0:32, :] = jnp.zeros((32, 256), BF16)

    from_mate.append(send(fh.at[pl.ds(0, 32)], fm.at[pl.ds(0, 32)], s_mate.at[2], r_mate.at[2], mate))
    head = jnp.concatenate([fh[0:16, :], fh[16:32, :]], axis=1)
    tail = jnp.concatenate([fh[16:32, :], jnp.zeros((16, 256), BF16)], axis=1)
    cat = jnp.concatenate([head, tail], axis=0)
    keep_halves(dot(cat, w1_ref[0:2].reshape(512, 1152)), ycor)
    gate(pre_ref[...] + widened(128, ycor), slice(0, 128))

    taps = jnp.concatenate([hid[a * 64 : a * 64 + 384, :] for a in range(3)], axis=1)
    away[...] = dot_nt(ord2_ref[pl.ds(pl.multiple_of((1 - core) * 256, 256), 256), :], taps).astype(BF16)
    from_mate.append(send(away, away_in, s_mate.at[3], r_mate.at[3], mate))

    near[1].wait_recv()

    @pl.when(tm == NTM - 1)
    def _():
        uh[...] = jnp.zeros((128, 128), BF16)

    from_mate.append(send(uh, uhm, s_mate.at[4], r_mate.at[4], mate))
    shifted(uh[...], 2, u9, 256)
    later = dot_nt(u9[256:384, :], w2_ref[0:2].reshape(256, 1152))
    back_ref[128:256, :] += later[:, 0:128]
    back_ref[192:256, :] += later[0:64, 128:256]
    dpre = (back_ref[...] * slope[...]).astype(BF16)
    pooled = dot(pool_ref[...], dpre).astype(BF16)
    for be in range(9):
        p9[32:96, be * 128 : be * 128 + 128] = pooled[be * 64 : be * 64 + 64]
    from_mate.append(send(p9.at[pl.ds(32, 64)], p9m, s_mate.at[5], r_mate.at[5], mate))
    turned[...] = dot_nt(ord2_ref[pl.ds(pl.multiple_of(core * 256, 256), 256), :], taps).astype(BF16)

    def put(chain, j, value):
        value = value.reshape(2, 8, 16, 128)
        for lo in range(2):
            sum_a[chain, lo * 2 + j % 2, j // 2] = value[lo, :CUT]
            sum_b[chain, j // 2, lo * 2 + j % 2] = value[lo, CUT:]

    def put_two(j, value):
        value = value.reshape(2, 8, 16, 128)
        for zz in range(NZ):
            c_sum[zz, j // 2, j % 2] = value[0, zz]
        d_sum[j // 2, j % 2] = value[1]

    def around(chain, swap):
        copies = []
        src_a, src_b, dst_a, dst_b = (mid_a, mid_b, mid_in_a, mid_in_b) if swap else (sum_a, sum_b, in_a, in_b)
        ssem, rsem = (s_two, r_two) if swap else (s_one, r_one)
        for k in (2, 1, 3, 0) if swap else (2, 1, 3):
            xd, yd = (x + k) % NX, (y + k) % NY
            ia, ib = (yd, xd) if swap else (xd, yd)
            to_a, to_b = (at(yy=yd), at(xx=xd)) if swap else (at(xx=xd), at(yy=yd))
            for src, dst, index, to, n in ((src_a, dst_a, ia, to_a, 2 * k - 2), (src_b, dst_b, ib, to_b, 2 * k - 1)):
                if swap:
                    held, parts, place = (sum_a, in_a, x) if src is src_a else (sum_b, in_b, y)
                    total = held[chain, place, index].astype(F32)
                    for m in range(3):
                        total += parts[chain, m, index].astype(F32)
                    src[chain, index] = total.astype(BF16)
                if k:
                    copies.append(
                        send(src.at[chain, index], dst.at[chain, k - 1], ssem.at[chain, n], rsem.at[chain, n], to)
                    )
        return copies

    def landed(copies):
        for copy in copies:
            copy.wait_recv()

    def added(own, parts, count):
        total = own.astype(F32)
        for k in range(count):
            total += parts[k].astype(F32)
        return total.astype(BF16)

    def stage_two(chain, copies):
        landed(copies)
        return around(chain, True)

    def stage_three(chain, copies):
        landed(copies)
        last[chain, 0:CUT] = added(mid_a[chain, y], mid_in_a.at[chain], 3)
        last[chain, CUT:NZ] = added(mid_b[chain, x], mid_in_b.at[chain], 3)
        copies = []
        for k in FAR_Z:
            zd = (z + k) % NZ
            copies.append(send(
                last.at[chain, zd], last_in.at[chain, k - 1], s_three.at[chain, k - 1], r_three.at[chain, k - 1], at(zz=zd)
            ))
        return copies

    def stage_four(chain, total):
        own[chain] = total
        gath[chain, tm] = total
        copies = []
        for k in FAR_TM:
            to = at_tm((tm + k) % NTM)
            copies.append(send(own.at[chain], gath.at[chain, tm], s_four.at[chain, k - 1], r_four.at[chain, k - 1], to))
        return copies

    def within(src, dst, ssem, rsem, lo):
        def copy(slot, index, to_hi):
            return pltpu.make_async_remote_copy(
                src_ref=src.at[index], dst_ref=dst.at[slot], send_sem=ssem.at[slot], recv_sem=rsem.at[slot],
                device_id=at(xx=lo * 2 + to_hi), device_id_type=MESH,
            )

        home = (copy(0, 1 - x_hi, 1 - x_hi),)
        abroad = (copy(1, x_hi, x_hi), copy(2, 1 - x_hi, 1 - x_hi))
        return home, abroad

    def each(condition, copies, method):
        @pl.when(condition)
        def _():
            for copy in copies:
                getattr(copy, method)()

    def over_y(src, dst, ssem, rsem):
        copies = []
        for k in range(1, NY):
            yd = (y + k) % NY
            copies.append(send(src.at[yd], dst.at[k - 1], ssem.at[k - 1], rsem.at[k - 1], at(yy=yd)))
        return copies

    from_mate[1].wait_recv()
    from_mate[2].wait_recv()
    feats = []
    mine = pl.ds(pl.multiple_of(core * 128, 128), 128)
    for a in range(3):
        rows = jnp.concatenate([fh[a * 16 : a * 16 + 64, :], fm[a * 16 : a * 16 + 64, :]], axis=0)
        feats.append(dot_nt(ord1_ref[mine, :], rows).astype(BF16))
    from_mate[5].wait_recv()
    units = []
    pools = jnp.concatenate([p9[32:96, :], p9m[...]], axis=0)
    for a in range(3):
        whole = dot(feats[a], pools)
        for be in range(9):
            units.append(whole[:, be * 128 : be * 128 + 128].reshape(16, 8, 128))
            if len(units) == 2:
                tile = (a * 9 + be) // 2
                put(tile // 8, tile % 8, jnp.concatenate(units, axis=1).astype(BF16))
                units = []
                if tile == 7:
                    f1 = around(0, False)
    from_mate[4].wait_recv()
    shifted(uhm[...], 2, u9m, 256)
    from_mate[3].wait_recv()
    for first in range(0, 9, 2):
        tap = slice(first * 128, min(first * 128 + 256, 1152))
        pair = dot(turned[...], u9[:, tap]) + dot(away_in[...], u9m[:, tap])
        pair = pair.astype(BF16)
        if first == 8:
            put(1, 6, pair)
        else:
            put_two(first, pair[:, 0:128])
            put_two(first + 1, pair[:, 128:256])

    d1 = over_y(d_sum, d_in, s_d1, r_d1)
    c1 = []
    for k in FAR_Z:
        zd = (z + k) % NZ
        c1.append(send(c_sum.at[zd], c_in.at[k - 1], s_c1.at[k - 1], r_c1.at[k - 1], at(zz=zd)))

    units.append(jnp.zeros((16, 8, 128), F32))
    put(1, 5, jnp.concatenate(units, axis=1).astype(BF16))
    put(1, 7, jnp.zeros((16, 16, 128), BF16))
    l1 = around(1, False)

    result = jnp.zeros((96, 256), F32)
    for a in range(3):
        result += dot_nt(p9[(2 - a) * 16 : (2 - a) * 16 + 96, :], w1_ref[a])
    part[...] = result
    near.append(send(part.at[pl.ds(0, 32)], part_in, s_near.at[2], r_near.at[2], prv))

    landed(d1)
    d_mid[...] = added(d_sum[y], d_in, 3)
    d_home, d_abroad = within(d_mid, d_mid_in, s_d2, r_d2, 1)
    each(x_lo == 1, d_home, "start")
    each(x_lo == 0, d_abroad, "start")
    f2 = stage_two(0, f1)
    l2 = stage_two(1, l1)
    landed(c1)
    c_mid[...] = added(c_sum[z], c_in, 7)
    c2 = over_y(c_mid, c_mid_in, s_c2, r_c2)
    f3 = stage_three(0, f2)

    d3 = []
    for k in FAR_Z:
        zd = (z + k) % NZ
        d3.append(pltpu.make_async_remote_copy(
            src_ref=d_end.at[zd], dst_ref=d_end_in.at[k - 1], send_sem=s_d3.at[k - 1], recv_sem=r_d3.at[k - 1],
            device_id=at(zz=zd), device_id_type=MESH,
        ))

    @pl.when(x_lo == 1)
    def _():
        for copy in d_home + d_abroad:
            copy.wait_recv()
        d_end[...] = added(d_mid[x_hi], d_mid_in, 3)
        for copy in d3:
            copy.start()

    l3 = stage_three(1, l2)
    landed(c2)
    c_end[...] = added(c_mid[y], c_mid_in, 3)
    c_home, c_abroad = within(c_end, c_end_in, s_c3, r_c3, 0)
    each(x_lo == 0, c_home, "start")
    each(x_lo == 1, c_abroad, "start")
    near[2].wait_recv()
    added_late = jnp.where(tm == NTM - 1, 0.0, part_in[...])
    fg_ref[0:32, :] = part[32:64, :].astype(BF16)
    fg_ref[32:64, :] = (part[64:96, :] + added_late).astype(BF16)
    landed(f3)
    f4 = stage_four(0, added(last[0, z], last_in.at[0], 7))

    @pl.when(x_lo == 0)
    def _():
        for copy in c_home + c_abroad:
            copy.wait_recv()
        final[...] = added(c_end[x_hi], c_end_in, 3)

    @pl.when(x_lo == 1)
    def _():
        for copy in d3:
            copy.wait_recv()
        final[...] = added(d_end[z], d_end_in, 7)

    e4 = stage_four(2, final[...])
    landed(l3)
    l4 = stage_four(1, added(last[1, z], last_in.at[1], 7))

    factor = 1.0 / 256.0
    landed(e4)
    for be in range(8):
        rows = gath[2, be].astype(F32) * factor
        for a in range(3):
            g2_ref[a * 9 + be] = rows[a * 4 : a * 4 + 4]
    landed(f4)
    for tile in range(15):
        if tile == 8:
            landed(l4)
        rows = gath[tile // 8, tile % 8].astype(F32) * factor
        if tile < 14:
            g1_ref[2 * tile] = rows[0:8]
        if tile < 13:
            g1_ref[2 * tile + 1] = rows[8:16]
        if tile == 14:
            for a in range(3):
                g2_ref[a * 9 + 8] = rows[a * 4 : a * 4 + 4]
    each(x_lo == 1, d_home + tuple(d3) + c_abroad, "wait_send")
    each(x_lo == 0, d_abroad + c_home, "wait_send")
    for copy in sent:
        copy.wait_send()


def store(*refs):
    sems = refs[6]
    copies = [pltpu.make_async_copy(refs[i], refs[3 + i], sems.at[i]) for i in range(3)]
    for copy in copies:
        copy.start()
    for copy in copies:
        copy.wait()


def on_device(features, upstream, weight_one, weight_two):
    dma, vmem = pltpu.SemaphoreType.DMA, pltpu.VMEM
    tile = lambda *lead: vmem(lead + (16, 128), BF16)
    pairs = lambda shape: [dma(shape), dma(shape)]
    scratch = [
        vmem((256, 128), BF16), vmem((3, 256, 1152), BF16), vmem((3, 128, 1152), BF16),
        vmem((256, 576), BF16), vmem((576, 256), BF16), vmem((256, 256), BF16), vmem((512, 384), BF16), dma((24,)),
        vmem((96, 256), BF16), vmem((128, 128), BF16), vmem((256, 128), BF16), vmem((128, 128), BF16),
        vmem((96, 256), BF16), vmem((96, 256), BF16),
        vmem((576, 256), BF16), vmem((576, 256), BF16), vmem((384, 1152), BF16), vmem((384, 1152), BF16),
        vmem((512, 128), BF16), vmem((128, 128), F32), vmem((256, 128), F32), vmem((256, 128), F32),
        vmem((128, 1152), BF16), vmem((64, 1152), BF16),
        vmem((256, 384), BF16), vmem((256, 384), BF16), vmem((256, 384), BF16),
        vmem((96, 256), F32), vmem((32, 256), F32),
        tile(2, NX, NY, CUT), tile(2, NY, NX, NZ - CUT), tile(2, 3, NY, CUT), tile(2, 3, NX, NZ - CUT),
        tile(2, NY, CUT), tile(2, NX, NZ - CUT), tile(2, 3, CUT), tile(2, 3, NZ - CUT),
        tile(2, NZ), tile(2, NZ - 1), tile(3), tile(3, NTM),
        tile(), tile(NZ, NY, 2), tile(NZ - 1, NY, 2), tile(NY, 2), tile(3, 2), tile(2), tile(3),
        tile(NY, 2, NZ), tile(3, 2, NZ), tile(2, NZ), tile(3, NZ), tile(NZ), tile(NZ - 1),
    ]
    scratch += pairs((3,)) + pairs((6,)) + pairs((2, 6)) * 2 + pairs((2, 7)) + pairs((3, 7))
    scratch += pairs((7,)) + pairs((3,)) * 4 + pairs((7,))
    spec = pl.BlockSpec(memory_space=pltpu.VMEM)
    shapes = (
        jax.ShapeDtypeStruct((64, 256), BF16),
        jax.ShapeDtypeStruct((27, 8, 128), F32),
        jax.ShapeDtypeStruct((27, 4, 128), F32),
    )
    results = pl.pallas_call(
        kernel,
        out_shape=shapes,
        in_specs=[pl.BlockSpec(memory_space=pltpu.HBM)] * 8,
        out_specs=(spec,) * 3,
        scratch_shapes=scratch,
        compiler_params=pltpu.CompilerParams(
            collective_id=0, has_side_effects=True, vmem_limit_bytes=24 * 1024 * 1024
        ),
    )(
        *(
            pltpu.with_memory_space_constraint(v, pltpu.HBM)
            for v in (
                features.reshape(64, 256),
                upstream.reshape(256, 128),
                weight_one.reshape(3, 9, 256, 128),
                weight_two.reshape(3, 9, 128, 128),
                *tables(),
            )
        )
    )
    fg, one, two = pl.pallas_call(
        store,
        out_shape=shapes,
        in_specs=[spec] * 3,
        out_specs=(pl.BlockSpec(memory_space=pltpu.HBM),) * 3,
        scratch_shapes=[dma((3,))],
    )(*(pltpu.with_memory_space_constraint(v, pltpu.VMEM) for v in results))
    return (
        fg.reshape(features.shape),
        one.reshape(3, 3, 3, 8, 128),
        two.reshape(3, 3, 3, 4, 128),
    )


def solution(mesh):
    wide = P("dp", "tm", None, None, None)
    cut = P(None, None, None, "dp", None)
    return jax.shard_map(
        on_device, mesh=mesh, in_specs=(wide, wide, P(), P()), out_specs=(wide, cut, cut), check_vma=False
    )
```
